256 devices in a mesh: dp: 32 (over z, x), head: 8 (over y, core).
Axes of the slice: x: 4, y: 4, z: 8, core: 2. Of those that a mesh axis runs over, the one named last changes fastest.
Arguments:
- queries: bfloat16 [5120, 128, 192], P(('dp', 'head')), may hold values from -6 to 6
- latents: bfloat16 [5120, 576], P('dp'), may hold values from -6 to 6
- cache_pool: bfloat16 [1024, 64, 576], P('dp'), may hold values from -6 to 6
- key_up: bfloat16 [128, 128, 512], P('head'), may hold values from -0.5 to 0.5
- value_up: bfloat16 [128, 512, 128], P('head'), may hold values from -0.25 to 0.25
- prefix_rank: int32 [1024, 1], P('dp'), may hold values from 0 to 31; in each aligned block of 32 rows (0 to 31, 32 to 63, ...) at most 2 rows name the same one
- prefix_block: int32 [1024], P('dp'), may hold values from 0 to 31
- decode_start: int32 [1024], P('dp'), may hold values from 0 to 1536
- decode_length: int32 [1024], P('dp'), may hold values from 1 to 512, as said below
Outputs:
- head_values: bfloat16 [5120, 128, 128], P(('dp', 'head'))
The draws below stay inside these ranges and needn't reach their ends.
Inputs may be any that keep to these rules, and one draw needn't show every extreme that they name: `prefix_rank`: among the 32 rows of one dp rank no rank is named more than 2 times. `decode_length`: every dp rank has a decode row of length 512.
All inputs are finite; a program needn't handle non-finite values.
Results may differ from the reference program's by a relative error of at most 0.0066.
Values may be sent and summed in bfloat16 or wider, within the bound.
A program may use at most 64 MiB of HBM per device.

```python
import math
import jax
import jax.numpy as jnp
import numpy as np
from jax import lax

H = 128
D_C = 512
D_R = 64
D_NOPE = 128
D_V = 128
CH = 128
DEC = 32
BLK = 64
NPB = 32
NBLK = 32
DMAX = 512
ROWS = 160
POOL = 2048
CAP = 2
N_DP = 32


def shared_pattern(key):
    sign_bits = jax.random.randint(jax.random.fold_in(key, 101), (D_R,), 0, 2)
    return (2 * sign_bits - 1).astype(jnp.float32)


def join_rotary(key, latent_part, pattern, lowest, highest):
    rotary_part = jax.random.uniform(key, latent_part.shape[:-1] + (D_R,), minval=lowest, maxval=highest) * pattern
    return jnp.concatenate([latent_part, rotary_part], axis=-1).astype(jnp.bfloat16)


def aligned_queries(key, base_values, pattern):
    picked = jax.random.randint(jax.random.fold_in(key, 5), (N_DP * ROWS, H), 0, 48)
    strengths = jnp.array([-6.0, -4.5, 4.5, 6.0], jnp.float32)
    strength = strengths[jnp.minimum(picked, 3)]
    rotary_part = jnp.where((picked < 4)[:, :, None], strength[:, :, None] * pattern, base_values[:, :, D_NOPE:])
    return jnp.concatenate([base_values[:, :, :D_NOPE], rotary_part], axis=2).astype(jnp.bfloat16)


def draw_queries(key, part):
    pattern = shared_pattern(key)
    key = jax.random.fold_in(key, 13)
    first_key, second_key = jax.random.split(key)
    full_shape = (N_DP * ROWS, H, D_NOPE + D_R)
    base_values = jnp.clip(jax.random.normal(first_key, full_shape), -6.0, 6.0)
    return aligned_queries(second_key, base_values, pattern)


def draw_latents(key, part):
    pattern = shared_pattern(key)
    key = jax.random.fold_in(key, 17)
    first_key, second_key = jax.random.split(key)
    latent_shape = (N_DP * ROWS, D_C)
    latent_part = jnp.clip(jax.random.normal(first_key, latent_shape), -6.0, 6.0)
    return join_rotary(second_key, latent_part, pattern, 3.0, 5.5)


def draw_cache_pool(key, part):
    pattern = shared_pattern(key)
    key = jax.random.fold_in(key, 19)
    first_key, second_key = jax.random.split(key)
    latent_shape = (N_DP * NBLK, BLK, D_C)
    latent_part = jnp.clip(jax.random.normal(first_key, latent_shape), -6.0, 6.0)
    return join_rotary(second_key, latent_part, pattern, 3.0, 5.5)


def draw_decode_length(key, part):
    key = jax.random.fold_in(key, 7)
    first_key, second_key = jax.random.split(key)
    lengths = jax.random.randint(first_key, (N_DP * DEC,), 1, DMAX + 1)
    chosen = jax.random.randint(second_key, (N_DP,), 0, DEC)
    indices = jnp.arange(N_DP * DEC)
    longest = indices % DEC == jnp.repeat(chosen, DEC, total_repeat_length=N_DP * DEC)
    return jnp.where(longest, DMAX, lengths).astype(jnp.int32)


def set_ends(values, key, least, top_value):
    spot = [jax.random.randint(jax.random.fold_in(key, axis), (), 0, length) for axis, length in enumerate(values.shape)]
    widest = values.shape.index(max(values.shape))
    beside = spot[:widest] + [(spot[widest] + 1) % values.shape[widest]] + spot[widest + 1:]
    return values.at[tuple(spot)].set(least).at[tuple(beside)].set(top_value)


def block_levels(key, dims, cuts, low, largest):
    def one(dim, shards_of):
        steps = jax.random.uniform(jax.random.fold_in(jax.random.fold_in(key, 6), dim), (shards_of,), jnp.float32, low / len(cuts), largest / len(cuts))
        return jnp.repeat(jnp.exp(steps), dims[dim] // shards_of).reshape((-1,) + (1,) * (len(dims) - dim - 1))

    level = one(*cuts[0])
    for cut in cuts[1:]:
        level = level * one(*cut)
    return level


def assign_block(stream_key, own, number, rows, number_of, top, limit, lean):
    sequence = jax.random.permutation(stream_key, number_of)
    heavy_load, common = shares(number_of, rows * top, limit, lean, True), shares(number_of, rows * top, limit, lean, False)
    places = jnp.arange(number_of)

    def named(sizes, rotation):
        used = int((sizes > 0).sum())
        fixed = max(1, used // 4)
        moved = fixed + (places - fixed + rotation * (used - fixed)) % max(1, number_of - fixed)
        return jnp.zeros((number_of,), jnp.int32).at[sequence[jnp.where(places < fixed, places, moved)]].set(jnp.asarray(sizes, jnp.int32))

    sizes = jnp.where(number % 4 == 0, named(heavy_load, number // 4), named(common, number - number // 4 - 1))
    mixed = jax.random.permutation(jax.random.fold_in(own, 3), number_of)
    giver, receiver = mixed[0:number_of // 2 * 2:2], mixed[1:number_of // 2 * 2:2]
    room = jnp.minimum(sizes[giver] - 1, limit - sizes[receiver]) // 2
    room = jnp.where((giver == sequence[0]) | (receiver == sequence[0]) | (sizes[receiver] == 0), 0, jnp.maximum(room, 0))
    moved = jax.random.randint(jax.random.fold_in(own, 4), (number_of // 2,), 0, 1 << 20) % (room + 1)
    sizes = sizes.at[giver].add(-moved).at[receiver].add(moved)
    labels = jnp.searchsorted(jnp.cumsum(sizes), jnp.arange(rows * top), side="right").astype(jnp.int32)
    table = labels.reshape(top, rows).T
    table = table[jax.random.permutation(jax.random.fold_in(own, 1), rows)]
    rotation = jax.random.randint(jax.random.fold_in(own, 2), (rows, 1), 0, top)
    return jnp.take_along_axis(table, (jnp.arange(top)[None, :] + rotation) % top, axis=1)


def shares(number_of, total, limit, lean, full):
    portions = [(1 << 20) // math.isqrt(standing ** lean) + 1 for standing in range(1, number_of + 1)]
    largest = limit if full else min(limit, max(-(-total // number_of), total * portions[0] // sum(portions)))
    least = 1 if total - largest >= number_of - 1 else 0
    counts, spare = [largest] + [least] * (number_of - 1), total - largest - least * (number_of - 1)
    while spare > 0:
        candidates = [i for i in range(1, number_of) if counts[i] < largest] or [i for i in range(1, number_of) if counts[i] < limit]
        pool, left = sum([portions[i] for i in candidates]), spare
        for i in candidates:
            more = min(limit - counts[i], max(1, left * portions[i] // pool), spare)
            counts[i] = counts[i] + more
            spare = spare - more
    return np.array(counts)


def gaussian(key, extent, spread, limit, cuts=(), kind=jnp.bfloat16):
    drawn = jax.random.normal(key, extent, jnp.float32) * spread
    if len(cuts) > 0:
        drawn = block_levels(key, extent, cuts, -0.22, 0.18) * drawn
    return jnp.clip(drawn, min=-limit, max=limit).astype(kind)


def setup_inputs(seed: int = 0) -> dict:
    splits = jax.random.split(jax.random.key(seed), 10)
    queries = draw_queries(jax.random.fold_in(splits[9], 71), 0)
    latents = draw_latents(jax.random.fold_in(splits[9], 71), 0)
    cache_pool = draw_cache_pool(jax.random.fold_in(splits[9], 71), 0)
    key_up = gaussian(splits[3], (H, D_NOPE, D_C), D_NOPE ** -0.5, 0.5, ((0, 8),))
    value_up = gaussian(splits[4], (H, D_C, D_V), D_C ** -0.5, 0.25, ((0, 8),))
    prefix_rank_keys = jax.random.split(jax.random.fold_in(splits[5], 1), (N_DP * NPB) // NPB)
    prefix_rank_turns = jax.random.permutation(jax.random.fold_in(splits[5], 3), (N_DP * NPB) // NPB)
    prefix_rank = jax.vmap(lambda own, number: assign_block(jax.random.fold_in(splits[5], 2), own, number, NPB, N_DP, 1, CAP, 2))(prefix_rank_keys, prefix_rank_turns).reshape((N_DP * NPB, 1))
    prefix_block = set_ends(jax.random.randint(splits[6], (N_DP * NPB,), 0, NBLK), jax.random.fold_in(splits[6], 1), 0, NBLK - 1).astype(jnp.int32)
    decode_start = set_ends(jax.random.randint(splits[7], (N_DP * DEC,), 0, POOL - DMAX + 1), jax.random.fold_in(splits[7], 1), 0, POOL - DMAX).astype(jnp.int32)
    decode_length = draw_decode_length(jax.random.fold_in(splits[9], 71), 0)
    return dict(queries=queries, latents=latents, cache_pool=cache_pool, key_up=key_up, value_up=value_up, prefix_rank=prefix_rank, prefix_block=prefix_block, decode_start=decode_start, decode_length=decode_length)


def softmax_mix(query_rows, key_rows, mask_bias, scale_value):
    scores = jnp.dot(query_rows, key_rows.T, preferred_element_type=jnp.float32) * scale_value + mask_bias
    row_peak = jnp.max(scores, axis=1, keepdims=True)
    raised = jnp.exp(scores - row_peak)
    denominator = jnp.sum(raised, axis=1, keepdims=True)
    weights = raised.astype(jnp.bfloat16)
    mixed_latent = jnp.dot(weights, key_rows[:, :D_C], preferred_element_type=jnp.float32)
    return mixed_latent / denominator


def reference(queries, latents, cache_pool, key_up, value_up, prefix_rank, prefix_block, decode_start, decode_length):
    scale_value = float(D_NOPE + D_R) ** -0.5
    width_all = D_C + D_R
    flat_cache = cache_pool.reshape(N_DP, POOL, width_all)
    holder_index = (prefix_rank[:, 0] * NBLK + prefix_block).astype(jnp.int32)
    prefix_all = cache_pool[holder_index].reshape(N_DP, NPB * BLK, width_all)
    prefix_length = NPB * BLK
    key_index = jnp.arange(prefix_length + CH)
    positions = jnp.arange(CH)
    prefill_bias = jnp.where((key_index[None, :] < prefix_length) | (key_index[None, :] - prefix_length <= positions[:, None]), 0.0, -jnp.inf).astype(jnp.float32)
    decode_index = jnp.arange(DMAX + 1)

    def one_rank(rank_item):
        rank_queries, rank_latents, rank_prefix, rank_cache, starts, lengths = rank_item
        absorbed = jnp.einsum("rhn,hnc->rhc", rank_queries[:, :, :D_NOPE].astype(jnp.float32), key_up.astype(jnp.float32)).astype(jnp.bfloat16)
        query_cat = jnp.concatenate([absorbed, rank_queries[:, :, D_NOPE:]], axis=2)
        prefill_keys = jnp.concatenate([rank_prefix, rank_latents[:CH]], axis=0)

        def prefill_head(head_query):
            return softmax_mix(head_query, prefill_keys, prefill_bias, scale_value)

        prefill_mixed = lax.map(prefill_head, jnp.transpose(query_cat[:CH], (1, 0, 2)))
        prefill_mixed = jnp.transpose(prefill_mixed, (1, 0, 2))

        def decode_one(decode_item):
            query_rows, first_row, length, own_key = decode_item
            window_rows = lax.dynamic_slice_in_dim(rank_cache, first_row.astype(jnp.int32), DMAX, 0)
            key_rows = jnp.concatenate([window_rows, own_key[None, :]], axis=0)
            visible = (decode_index < length) | (decode_index == DMAX)
            mask_bias = jnp.where(visible, 0.0, -jnp.inf).astype(jnp.float32)[None, :]
            return softmax_mix(query_rows, key_rows, mask_bias, scale_value)

        decode_mixed = lax.map(decode_one, (query_cat[CH:], starts, lengths, rank_latents[CH:]))
        mixed_latent = jnp.concatenate([prefill_mixed, decode_mixed], axis=0).astype(jnp.bfloat16)
        return jnp.einsum("rhc,hcv->rhv", mixed_latent.astype(jnp.float32), value_up.astype(jnp.float32)).astype(jnp.bfloat16)

    outputs = lax.map(one_rank, (queries.reshape(N_DP, ROWS, H, D_NOPE + D_R), latents.reshape(N_DP, ROWS, width_all), prefix_all, flat_cache, decode_start.reshape(N_DP, DEC), decode_length.reshape(N_DP, DEC)))
    return outputs.reshape(N_DP * ROWS, H, D_V)
```

```python
import functools
import math

import jax
import jax.numpy as jnp
from jax import lax
from jax.experimental import pallas as pl
from jax.experimental.pallas import tpu as pltpu
from jax.sharding import PartitionSpec as P

MESH = pl.DeviceIdType.MESH
CAP = 2
F32 = jnp.float32
BF16 = jnp.bfloat16
HIDDEN = -1e30


def iota(shape, dim):
    return lax.broadcasted_iota(jnp.int32, shape, dim)


def wait_bytes(ref, sem):
    pltpu.make_async_copy(ref, ref, sem).wait()


def gather_kernel(
    q_ref, cache_ref, rank_ref, block_ref, qg_ref, keys_ref,
    table, ids, rows_here, outgoing, arrived, chunk,
    local_sem, id_send, id_recv, q_send, q_recv, row_send, row_recv, ag_send, ag_recv,
):
    nd, nh = lax.axis_size("dp"), lax.axis_size("head")
    me, hd = lax.axis_index("dp"), lax.axis_index("head")
    chip, core = hd // 2, hd % 2
    blocks, block_rows, width = cache_ref.shape
    part = block_rows // nh
    pair = CAP * part
    q_rows = q_ref.shape[0]
    heads = qg_ref.shape[1]
    reqs = rank_ref.shape[0]
    sibling = chip * 2 + 1 - core

    rows_copy = pltpu.make_async_copy(
        cache_ref.at[:, pl.ds(pl.multiple_of(chip * pair, pair), pair), :], rows_here, local_sem.at[0]
    )
    rows_copy.start()
    barrier = pltpu.get_barrier_semaphore()

    def greet_dp(step, carry):
        peer = lax.rem(me + step, nd)
        pl.semaphore_signal(barrier, inc=1, device_id=(peer, hd), device_id_type=MESH)
        return carry

    def greet_head(step, carry):
        peer = lax.rem(hd + step, nh)
        pl.semaphore_signal(barrier, inc=1, device_id=(me, peer), device_id_type=MESH)
        return carry

    lax.fori_loop(1, nd, greet_dp, 0)
    lax.fori_loop(1, nh, greet_head, 0)

    rank_col = rank_ref[...].astype(F32)
    row_i, col_i = iota((reqs, reqs), 0), iota((reqs, reqs), 1)
    rank_row = jnp.sum(jnp.where(row_i == col_i, rank_col, 0.0), axis=0, keepdims=True)
    same = rank_col == rank_row
    within_row = jnp.sum(jnp.where(same & (row_i < col_i), 1.0, 0.0), axis=0, keepdims=True)
    within_col = jnp.sum(jnp.where(same & (col_i < row_i), 1.0, 0.0), axis=1, keepdims=True)
    block_row = block_ref[...].astype(F32) + 1.0
    hit = rank_row == iota((nd, reqs), 0).astype(F32)
    want0 = jnp.sum(jnp.where(hit & (within_row == 0.0), block_row, 0.0), axis=1, keepdims=True) - 1.0
    want1 = jnp.sum(jnp.where(hit & (within_row == 1.0), block_row, 0.0), axis=1, keepdims=True) - 1.0
    lane = iota((nd, 128), 1)
    table[:, 0, :] = jnp.where(lane == 0, want0, jnp.where(lane == 1, want1, 0.0))

    pl.semaphore_wait(barrier, nd - 1 + nh - 1)

    def send_ids(step, carry):
        peer = lax.rem(me + step, nd)
        pltpu.make_async_remote_copy(
            src_ref=table.at[peer], dst_ref=ids.at[me], send_sem=id_send, recv_sem=id_recv,
            device_id=(peer, hd), device_id_type=MESH,
        ).start()
        return carry

    lax.fori_loop(1, nd, send_ids, 0)
    own_ids = pltpu.make_async_copy(table.at[me], ids.at[me], local_sem.at[1])
    own_ids.start()

    def send_q(step, carry):
        peer = lax.rem(hd + step, nh)
        pltpu.make_async_remote_copy(
            src_ref=q_ref.at[:, pl.ds(pl.multiple_of(peer * heads, heads), heads), :],
            dst_ref=qg_ref.at[pl.ds(hd * q_rows, q_rows)], send_sem=q_send, recv_sem=q_recv,
            device_id=(me, peer), device_id_type=MESH,
        ).start()
        return carry

    lax.fori_loop(1, nh, send_q, 0)
    own_q = pltpu.make_async_copy(
        q_ref.at[:, pl.ds(pl.multiple_of(hd * heads, heads), heads), :],
        qg_ref.at[pl.ds(hd * q_rows, q_rows)], local_sem.at[2],
    )
    own_q.start()

    own_ids.wait()
    wait_bytes(ids.at[pl.ds(0, nd - 1)], id_recv)
    rows_copy.wait()
    total = nd * pair
    expand = (iota((total, nd), 0) // pair == iota((total, nd), 1)).astype(BF16)
    asked = jnp.dot(expand, ids[:, 0, :].astype(BF16), preferred_element_type=F32)
    row_c = iota((total, 1), 0)
    second = lax.rem(row_c // part, CAP) == 1
    wanted = jnp.where(second, asked[:, 1:2], asked[:, 0:1])
    offset = (lax.rem(row_c, part) + core * part).astype(F32)
    target = jnp.where(wanted < 0.0, -1e6, wanted * pair) + offset
    pick = (iota((total, blocks * pair), 1).astype(F32) == target).astype(BF16)
    outgoing[...] = jnp.dot(
        pick, rows_here[...].reshape(blocks * pair, width), preferred_element_type=F32
    ).astype(BF16).reshape(nd, pair, width)

    def send_rows(step, carry):
        peer = lax.rem(me + step, nd)
        pltpu.make_async_remote_copy(
            src_ref=outgoing.at[peer], dst_ref=arrived.at[me], send_sem=row_send, recv_sem=row_recv,
            device_id=(peer, hd), device_id_type=MESH,
        ).start()
        return carry

    lax.fori_loop(1, nd, send_rows, 0)
    own_rows = pltpu.make_async_copy(outgoing.at[me], arrived.at[me], local_sem.at[3])
    own_rows.start()

    spread = (iota((reqs * part, reqs), 0) // part == iota((reqs * part, reqs), 1)).astype(BF16)
    place = jnp.broadcast_to(rank_col * CAP + within_col, (reqs, 128)).astype(BF16)
    place = jnp.dot(spread, place, preferred_element_type=F32)[:, 0:1]
    place = place * part + lax.rem(iota((reqs * part, 1), 0), part).astype(F32)
    choose = (iota((reqs * part, total), 1).astype(F32) == place).astype(BF16)
    own_rows.wait()
    wait_bytes(arrived.at[pl.ds(0, nd - 1)], row_recv)
    chunk[...] = jnp.dot(
        choose, arrived[...].reshape(total, width), preferred_element_type=F32
    ).astype(BF16)

    def share(source, index, peer, slot):
        return pltpu.make_async_remote_copy(
            src_ref=source, dst_ref=keys_ref.at[index], send_sem=ag_send.at[slot],
            recv_sem=ag_recv.at[index], device_id=(me, peer), device_id_type=MESH,
        )

    chips = nh // 2
    for step in range(1, chips):
        share(chunk, hd, lax.rem(hd + 2 * step, nh), step).start()
    share(chunk, hd, sibling, 0).start()
    own_chunk = pltpu.make_async_copy(chunk, keys_ref.at[hd], local_sem.at[4])
    own_chunk.start()
    for step in range(1, chips):
        source = lax.rem(hd - 2 * step + nh, nh)
        share(chunk, source, sibling, 0).wait_recv()
        share(keys_ref.at[source], source, sibling, chips + step).start()
    for step in range(chips):
        source = lax.rem(sibling + 2 * step, nh)
        share(chunk, source, sibling, 0).wait_recv()

    own_chunk.wait()
    for step in range(chips):
        share(chunk, hd, sibling, step).wait_send()
    for step in range(1, chips):
        share(chunk, hd, sibling, chips + step).wait_send()
    own_q.wait()
    wait_bytes(qg_ref.at[pl.ds(0, (nh - 1) * q_rows)], q_recv)
    wait_bytes(qg_ref.at[pl.ds(0, (nh - 1) * q_rows)], q_send)
    wait_bytes(outgoing.at[pl.ds(0, nd - 1)], row_send)
    wait_bytes(table.at[pl.ds(0, nd - 1)], id_send)


def attend_kernel(
    qg_ref, latents_ref, cache_ref, keys_ref, key_up_ref, value_up_ref, start_ref, length_ref, out_ref,
    nope, rope, query_p, query_d, mixed_p, mixed_d, values, seen,
):
    rows, heads, q_width = qg_ref.shape
    nope_dim, latent = key_up_ref.shape[1], key_up_ref.shape[2]
    rope_dim = q_width - nope_dim
    dec = start_ref.shape[1]
    pre = rows - dec
    width = latent + rope_dim
    pool = cache_ref.shape[0]
    exponent = float(q_width) ** (-0.5) * math.log2(math.e)

    flat = qg_ref[...].reshape(rows * heads, q_width).astype(F32)
    nope[...] = flat[:, :nope_dim]
    rope[:, :rope_dim] = flat[:, nope_dim:]
    for h in range(heads):
        picked = nope[pl.ds(h, rows, stride=heads), :].astype(BF16)
        absorbed = jnp.dot(picked, key_up_ref[h], preferred_element_type=F32).astype(BF16)
        turned = rope[pl.ds(h, rows, stride=heads), :].astype(BF16)[:, :rope_dim]
        query_p[pl.ds(h * pre, pre), :latent] = absorbed[:pre]
        query_p[pl.ds(h * pre, pre), latent:] = turned[:pre]
        query_d[pl.ds(h * dec, dec), :latent] = absorbed[pre:]
        query_d[pl.ds(h * dec, dec), latent:] = turned[pre:]

    def scores(query, keys):
        return lax.dot_general(query, keys, (((1,), (1,)), ((), ())), preferred_element_type=F32)

    def mix(first, keys, second, local):
        peak = jnp.maximum(
            jnp.max(first, axis=1, keepdims=True), jnp.max(second, axis=1, keepdims=True)
        ) * exponent
        raised1 = jnp.exp2(first * exponent - peak)
        raised2 = jnp.exp2(second * exponent - peak)
        total = jnp.sum(raised1, axis=1, keepdims=True) + jnp.sum(raised2, axis=1, keepdims=True)
        mixed = jnp.dot(raised1.astype(BF16), keys[:, :latent], preferred_element_type=F32)
        mixed += jnp.dot(raised2.astype(BF16), local[:, :latent], preferred_element_type=F32)
        return (mixed / total).astype(BF16)

    size = 2 * pre

    def prefill_block(index, carry):
        at = pl.ds(pl.multiple_of(index * size, size), size)
        query = query_p[at, :]
        local = latents_ref[:pre, :]
        keys = keys_ref[...]
        first = scores(query, keys)
        second = scores(query, local)
        position = lax.rem(iota((size, pre), 0), pre)
        second = jnp.where(iota((size, pre), 1) <= position, second, HIDDEN)
        mixed_p[at, :] = mix(first, keys, second, local)
        return carry

    lax.fori_loop(0, heads * pre // size, prefill_block, 0)

    eye = iota((dec, dec), 0) == iota((dec, dec), 1)
    start = jnp.sum(jnp.where(eye, start_ref[...].astype(F32), 0.0), axis=1, keepdims=True)
    length = jnp.sum(jnp.where(eye, length_ref[...].astype(F32), 0.0), axis=1, keepdims=True)
    place = iota((dec, pool), 1).astype(F32) - start
    seen[...] = jnp.where((place >= 0.0) & (place < length), 0.0, HIDDEN)
    group = size // dec

    def decode_block(index, carry):
        at = pl.ds(pl.multiple_of(index * size, size), size)
        query = query_d[at, :]
        local = latents_ref[rows - pre:, :]
        cache = cache_ref[...]
        first = (scores(query, cache).reshape(group, dec, pool) + seen[...][None]).reshape(size, pool)
        second = scores(query, local)
        own = lax.rem(iota((size, pre), 0), dec) + (pre - dec)
        second = jnp.where(iota((size, pre), 1) == own, second, HIDDEN)
        mixed_d[at, :] = mix(first, cache, second, local)
        return carry

    lax.fori_loop(0, heads * dec // size, decode_block, 0)

    for h in range(heads):
        values[pl.ds(h, pre, stride=heads), :] = jnp.dot(
            mixed_p[pl.ds(h * pre, pre), :], value_up_ref[h], preferred_element_type=F32
        )
        values[pl.ds(pre * heads + h, dec, stride=heads), :] = jnp.dot(
            mixed_d[pl.ds(h * dec, dec), :], value_up_ref[h], preferred_element_type=F32
        )
    out_ref[...] = values[...].astype(BF16).reshape(out_ref.shape)


def return_kernel(values_ref, out_ref, local_sem, send_sem, recv_sem):
    nh = lax.axis_size("head")
    me, hd = lax.axis_index("dp"), lax.axis_index("head")
    heads = values_ref.shape[1]
    rows = out_ref.shape[0]
    barrier = pltpu.get_barrier_semaphore()

    def greet(step, carry):
        peer = lax.rem(hd + step, nh)
        pl.semaphore_signal(barrier, inc=1, device_id=(me, peer), device_id_type=MESH)
        return carry

    lax.fori_loop(1, nh, greet, 0)
    here = pl.ds(pl.multiple_of(hd * heads, heads), heads)
    own = pltpu.make_async_copy(values_ref.at[pl.ds(hd * rows, rows)], out_ref.at[:, here, :], local_sem)
    own.start()
    pl.semaphore_wait(barrier, nh - 1)

    def send(step, carry):
        peer = lax.rem(hd + step, nh)
        pltpu.make_async_remote_copy(
            src_ref=values_ref.at[pl.ds(peer * rows, rows)], dst_ref=out_ref.at[:, here, :],
            send_sem=send_sem, recv_sem=recv_sem, device_id=(me, peer), device_id_type=MESH,
        ).start()
        return carry

    lax.fori_loop(1, nh, send, 0)
    own.wait()
    wait_bytes(values_ref.at[pl.ds(0, (nh - 1) * rows)], send_sem)
    wait_bytes(values_ref.at[pl.ds(0, (nh - 1) * rows)], recv_sem)


def body(
    queries, latents, cache_pool, key_up, value_up, prefix_rank, prefix_block, decode_start, decode_length
):
    nd, nh = lax.axis_size("dp"), lax.axis_size("head")
    q_rows, all_heads, q_width = queries.shape
    heads = all_heads // nh
    rows = q_rows * nh
    blocks, block_rows, width = cache_pool.shape
    part = block_rows // nh
    pair = CAP * part
    reqs = prefix_block.shape[0]
    latent = key_up.shape[2]
    dec = decode_start.shape[0]
    pre = rows - dec
    v_dim = value_up.shape[2]
    anywhere = pl.BlockSpec(memory_space=pl.ANY)
    vmem = pl.BlockSpec(memory_space=pltpu.VMEM)
    dma = pltpu.SemaphoreType.DMA

    grouped, keys = pl.pallas_call(
        gather_kernel,
        out_shape=[
            jax.ShapeDtypeStruct((rows, heads, q_width), BF16),
            jax.ShapeDtypeStruct((nh, reqs * part, width), BF16),
        ],
        in_specs=[anywhere, anywhere, vmem, vmem],
        out_specs=[anywhere, anywhere],
        scratch_shapes=[
            pltpu.VMEM((nd, 1, 128), F32),
            pltpu.VMEM((nd, 1, 128), F32),
            pltpu.VMEM((blocks, pair, width), BF16),
            pltpu.VMEM((nd, pair, width), BF16),
            pltpu.VMEM((nd, pair, width), BF16),
            pltpu.VMEM((reqs * part, width), BF16),
            dma((5,)), dma, dma, dma, dma, dma, dma, dma((nh,)), dma((nh,)),
        ],
        compiler_params=pltpu.CompilerParams(
            collective_id=0, has_side_effects=True, vmem_limit_bytes=32 * 2**20
        ),
        name="gather",
    )(queries, cache_pool, prefix_rank, prefix_block.reshape(1, reqs))

    values = pl.pallas_call(
        attend_kernel,
        out_shape=jax.ShapeDtypeStruct((rows, heads, v_dim), BF16),
        in_specs=[vmem] * 8,
        out_specs=vmem,
        scratch_shapes=[
            pltpu.VMEM((rows * heads, 128), F32),
            pltpu.VMEM((rows * heads, 128), F32),
            pltpu.VMEM((pre * heads, width), BF16),
            pltpu.VMEM((dec * heads, width), BF16),
            pltpu.VMEM((pre * heads, latent), BF16),
            pltpu.VMEM((dec * heads, latent), BF16),
            pltpu.VMEM((rows * heads, v_dim), F32),
            pltpu.VMEM((dec, blocks * block_rows), F32),
        ],
        compiler_params=pltpu.CompilerParams(vmem_limit_bytes=56 * 2**20),
        name="attend",
    )(
        grouped, latents, cache_pool.reshape(blocks * block_rows, width),
        keys.reshape(nh * reqs * part, width), key_up, value_up,
        decode_start.reshape(1, dec), decode_length.reshape(1, dec),
    )

    return pl.pallas_call(
        return_kernel,
        out_shape=jax.ShapeDtypeStruct((q_rows, all_heads, v_dim), BF16),
        in_specs=[anywhere],
        out_specs=anywhere,
        scratch_shapes=[dma, dma, dma],
        compiler_params=pltpu.CompilerParams(collective_id=1, has_side_effects=True),
        name="give_back",
    )(values)


def solution(mesh):
    return jax.shard_map(
        body,
        mesh=mesh,
        in_specs=(
            P(("dp", "head"), None, None),
            P("dp", None),
            P("dp", None, None),
            P("head", None, None),
            P("head", None, None),
            P("dp", None),
            P("dp"),
            P("dp"),
            P("dp"),
        ),
        out_specs=P(("dp", "head"), None, None),
        check_vma=False,
    )
```

```python
import functools
import math

import jax
import jax.numpy as jnp
from jax import lax
from jax.experimental import pallas as pl
from jax.experimental.pallas import tpu as pltpu
from jax.sharding import PartitionSpec as P

MESH = pl.DeviceIdType.MESH
CAP = 2
F32 = jnp.float32
BF16 = jnp.bfloat16
HIDDEN = -1e30


def iota(shape, dim):
    return lax.broadcasted_iota(jnp.int32, shape, dim)


def wait_bytes(ref, sem):
    pltpu.make_async_copy(ref, ref, sem).wait()


def gather_lists(rank_row, block_row, nd):
    reqs = rank_row.shape[1]
    half = reqs // 2
    row_i, col_i = iota((reqs, reqs), 0), iota((reqs, reqs), 1)

    def down(mask, values=1.0):
        return jnp.sum(jnp.where(mask, values, 0.0), axis=0, keepdims=True)

    def across(mask, values=1.0):
        return jnp.sum(jnp.where(mask, values, 0.0), axis=1, keepdims=True)

    rank_col = across(row_i == col_i, rank_row)
    same = rank_col == rank_row
    slot_row = down(same & (row_i < col_i))
    slot_col = across(same & (col_i < row_i))
    hit = rank_row == iota((nd, reqs), 0).astype(F32)
    want0 = across(hit & (slot_row == 0.0), block_row + 1.0) - 1.0
    want1 = across(hit & (slot_row == 1.0), block_row + 1.0) - 1.0
    spot_row = down((row_i < col_i) & (slot_col == 0.0))
    spot_col = across((col_i < row_i) & (slot_row == 0.0))
    early_row = (slot_row == 0.0) & (spot_row < half)
    early_col = (slot_col == 0.0) & (spot_col < half)
    late_row = down((row_i < col_i) & jnp.logical_not(early_col))
    order = iota((half, reqs), 0).astype(F32)
    early = across((order == spot_row) & early_row, rank_row)
    late = across((order == late_row) & jnp.logical_not(early_row), slot_row * nd + rank_row)
    return want0, want1, early, late


def spread_rows(column, part):
    count = column.shape[0]
    expand = (iota((count * part, count), 0) // part == iota((count * part, count), 1)).astype(BF16)
    wide = jnp.broadcast_to(column, (count, 128)).astype(BF16)
    spread = jnp.dot(expand, wide, preferred_element_type=F32)[:, 0:1]
    return spread * part + lax.rem(iota((count * part, 1), 0), part).astype(F32)


def pick_rows(target, first, source):
    total = source.shape[0]
    pick = (iota((target.shape[0], total), 1).astype(F32) + first == target).astype(BF16)
    return jnp.dot(pick, source, preferred_element_type=F32)


def scores(query, keys):
    return lax.dot_general(query, keys, (((1,), (1,)), ((), ())), preferred_element_type=F32)


def kernel(
    q_ref, latents_hbm, cache_hbm, key_up_hbm, value_up_hbm, rank_ref, block_ref, start_ref, length_ref,
    out_ref,
    q_in, latents, cache, key_up, value_up, rows_here, table, ids,
    nope_out, rope_out, nope_in, rope_in, nope, rope, out0, out1, in0, in1, keys_a, keys_b,
    query_p, query_d, mixed_p, mixed_d, values, values_out, seen, acc, peak, total,
    local_sem, id_send, id_recv, nope_send, nope_recv, rope_send, rope_recv,
    send0, recv0, send1, recv1, a_send, a_recv, b_send, b_recv, out_send, out_recv, own_sem,
):
    nd, nh = lax.axis_size("dp"), lax.axis_size("head")
    chips = nh // 2
    me, hd = lax.axis_index("dp"), lax.axis_index("head")
    chip, core = hd // 2, hd % 2
    sibling = chip * 2 + 1 - core
    blocks, block_rows, width = cache_hbm.shape
    part = block_rows // nh
    pair = CAP * part
    q_rows, q_width, all_heads = q_ref.shape
    heads, nope_dim, latent = key_up_hbm.shape
    rope_dim = q_width - nope_dim
    rows = q_rows * nh
    reqs = rank_ref.shape[1]
    dec = start_ref.shape[1]
    pre = rows - dec
    pool = blocks * block_rows
    exponent = float(q_width) ** (-0.5) * math.log2(math.e)
    front = chips - 1

    def place_of(device):
        moved = jnp.where(device % 2 == 0, device // 2, front + device // 2)
        return jnp.where(device < 2 * front, moved, device) * q_rows

    loads = [
        pltpu.make_async_copy(source, dest, local_sem.at[i])
        for i, (source, dest) in enumerate([
            (q_ref, q_in),
            (cache_hbm.at[:, pl.ds(pl.multiple_of(chip * pair, pair), pair), :], rows_here),
            (key_up_hbm, key_up), (latents_hbm, latents), (cache_hbm, cache), (value_up_hbm, value_up),
        ])
    ]
    for load in loads:
        load.start()
    barrier = pltpu.get_barrier_semaphore()

    def greet_dp(step, carry):
        pl.semaphore_signal(barrier, inc=1, device_id=(lax.rem(me + step, nd), hd), device_id_type=MESH)
        return carry

    def greet_head(step, carry):
        pl.semaphore_signal(barrier, inc=1, device_id=(me, lax.rem(hd + step, nh)), device_id_type=MESH)
        return carry

    lax.fori_loop(1, nd, greet_dp, 0)
    lax.fori_loop(1, nh, greet_head, 0)

    want0, want1, early, late = gather_lists(
        rank_ref[...].astype(F32), block_ref[...].astype(F32), nd
    )
    lane = iota((nd, 128), 1)
    table[:, 0, :] = jnp.where(lane == 0, want0, jnp.where(lane == 1, want1, 0.0))

    pl.semaphore_wait(barrier, nd - 1 + nh - 1)

    def send_ids(step, carry):
        peer = lax.rem(me + step, nd)
        pltpu.make_async_remote_copy(
            src_ref=table.at[peer], dst_ref=ids.at[me], send_sem=id_send, recv_sem=id_recv,
            device_id=(peer, hd), device_id_type=MESH,
        ).start()
        return carry

    lax.fori_loop(1, nd, send_ids, 0)
    own_ids = pltpu.make_async_copy(table.at[me], ids.at[me], own_sem.at[0])
    own_ids.start()

    loads[0].wait()
    half_heads = heads // 2

    def turn(step, carry):
        turned = []
        for k in range(2):
            one = jnp.transpose(q_in[2 * step + k].astype(F32), (1, 0))
            nope_out[2 * step + k] = one[:, :nope_dim].astype(BF16)
            both = one[:, nope_dim:].reshape(nh, 2, half_heads, rope_dim)
            turned.append(jnp.concatenate([both[:, 0], both[:, 1]], axis=2))
        at = pl.ds(pl.multiple_of(step * 2 * half_heads, 2 * half_heads), 2 * half_heads)
        rope_out[:, at, :] = jnp.concatenate(turned, axis=1).astype(BF16)
        return carry

    lax.fori_loop(0, q_rows // 2, turn, 0)

    here = place_of(hd)

    def q_copies(peer, remote):
        nope_from = nope_out.at[:, pl.ds(pl.multiple_of(peer * heads, heads), heads), :]
        nope_to = nope_in.at[pl.ds(here, q_rows)]
        rope_to = rope_in.at[here // q_rows]
        if not remote:
            return [
                pltpu.make_async_copy(nope_from, nope_to, own_sem.at[1]),
                pltpu.make_async_copy(rope_out.at[peer], rope_to, own_sem.at[2]),
            ]
        return [
            pltpu.make_async_remote_copy(
                src_ref=nope_from, dst_ref=nope_to, send_sem=nope_send, recv_sem=nope_recv,
                device_id=(me, peer), device_id_type=MESH,
            ),
            pltpu.make_async_remote_copy(
                src_ref=rope_out.at[peer], dst_ref=rope_to, send_sem=rope_send, recv_sem=rope_recv,
                device_id=(me, peer), device_id_type=MESH,
            ),
        ]

    def send_q(step, carry):
        for copy in q_copies(lax.rem(hd + step, nh), True):
            copy.start()
        return carry

    lax.fori_loop(1, nh, send_q, 0)
    own_q = q_copies(hd, False)
    for copy in own_q:
        copy.start()

    loads[1].wait()
    own_ids.wait()
    wait_bytes(ids.at[pl.ds(0, nd - 1)], id_recv)
    expand = (iota((nd * part, nd), 0) // part == iota((nd * part, nd), 1)).astype(BF16)
    asked = jnp.dot(expand, ids[:, 0, :].astype(BF16), preferred_element_type=F32)
    offset = (lax.rem(iota((nd * part, 1), 0), part) + core * part).astype(F32)

    def row_copy(source, dest, send_sem, recv_sem, peer):
        return pltpu.make_async_remote_copy(
            src_ref=source.at[peer], dst_ref=dest.at[me], send_sem=send_sem, recv_sem=recv_sem,
            device_id=(peer, hd), device_id_type=MESH,
        )

    own_rows = []
    for slot, (source, dest, send_sem, recv_sem) in enumerate(
        [(out0, in0, send0, recv0), (out1, in1, send1, recv1)]
    ):
        wanted = asked[:, slot:slot + 1]
        target = jnp.where(wanted < 0.0, -1e6, wanted * pair) + offset
        picked = pick_rows(target, 0.0, rows_here[...].reshape(blocks * pair, width))
        source[...] = picked.astype(BF16).reshape(nd, part, width)

        def send_rows(step, carry, source=source, dest=dest, send_sem=send_sem, recv_sem=recv_sem):
            row_copy(source, dest, send_sem, recv_sem, lax.rem(me + step, nd)).start()
            return carry

        lax.fori_loop(1, nd, send_rows, 0)
        own = pltpu.make_async_copy(source.at[me], dest.at[me], own_sem.at[3 + slot])
        own.start()
        own_rows.append(own)

    for copy in own_q:
        copy.wait()
    loads[2].wait()
    wait_bytes(nope_in.at[pl.ds(0, rows - q_rows)], nope_recv)
    wait_bytes(rope_in.at[pl.ds(0, nh - 1)], rope_recv)
    nope[...] = nope_in[...].reshape(rows * heads, nope_dim).astype(F32)
    rope[...] = rope_in[...].reshape(rows * half_heads, 2 * rope_dim).astype(F32)
    part_rows = pre // 2

    def put_query(h, columns, value):
        for side in range(2):
            at = pl.ds((side * heads + h) * part_rows, part_rows)
            query_p[at, columns] = value[side * part_rows:(side + 1) * part_rows]
        query_d[pl.ds(h * dec, dec), columns] = value[pre:]

    for h in range(heads):
        picked = nope[pl.ds(h, rows, stride=heads), :].astype(BF16)
        absorbed = jnp.dot(picked, key_up[h], preferred_element_type=F32).astype(BF16)
        put_query(h, slice(0, latent), absorbed)
    for h in range(half_heads):
        both = rope[pl.ds(h, rows, stride=half_heads), :].astype(BF16)
        put_query(h, slice(latent, width), both[:, :rope_dim])
        put_query(h + half_heads, slice(latent, width), both[:, rope_dim:])

    def share(keys, send_sem, recv_sem, index, peer, slot):
        return pltpu.make_async_remote_copy(
            src_ref=keys.at[index], dst_ref=keys.at[index], send_sem=send_sem.at[slot],
            recv_sem=recv_sem.at[index], device_id=(me, peer), device_id_type=MESH,
        )

    def share_own(*gang):
        for step in range(1, chips):
            share(*gang, hd, lax.rem(hd + 2 * step, nh), step).start()
        share(*gang, hd, sibling, 0).start()

    def share_on(*gang):
        for step in range(1, chips):
            source = lax.rem(hd - 2 * step + nh, nh)
            share(*gang, source, sibling, 0).wait_recv()
            share(*gang, source, sibling, chips + step).start()

    def share_end(*gang):
        for step in range(chips):
            share(*gang, lax.rem(sibling + 2 * step, nh), sibling, 0).wait_recv()

    def share_sent(*gang):
        for slot in [*range(chips), *range(chips + 1, 2 * chips)]:
            share(*gang, hd, sibling, slot).wait_send()

    gang_a = (keys_a, a_send, a_recv)
    gang_b = (keys_b, b_send, b_recv)

    own_rows[0].wait()
    wait_bytes(in0.at[pl.ds(0, nd - 1)], recv0)
    first_rows = in0[...].reshape(nd * part, width)
    keys_a[hd] = pick_rows(spread_rows(early, part), 0.0, first_rows).astype(BF16)
    share_own(*gang_a)

    loads[3].wait()
    loads[4].wait()
    eye = iota((dec, dec), 0) == iota((dec, dec), 1)
    start = jnp.sum(jnp.where(eye, start_ref[...].astype(F32), 0.0), axis=1, keepdims=True)
    length = jnp.sum(jnp.where(eye, length_ref[...].astype(F32), 0.0), axis=1, keepdims=True)
    place = iota((dec, pool), 1).astype(F32) - start
    seen[...] = jnp.where((place >= 0.0) & (place < length), 0.0, HIDDEN)
    step_blocks = blocks // 4
    step_keys = step_blocks * block_rows
    size_d = heads * dec // 2

    def decode_block(index, carry):
        at = pl.ds(pl.multiple_of(index * size_d, size_d), size_d)
        query = query_d[at, :]
        local = latents[rows - pre:, :]
        own = lax.rem(iota((size_d, pre), 0), dec) + (pre - dec)
        kept = [jnp.where(iota((size_d, pre), 1) == own, scores(query, local), HIDDEN)]
        held = [local]
        for j in range(4):
            keys = cache[j * step_blocks:(j + 1) * step_blocks].reshape(step_keys, width)
            one = scores(query, keys).reshape(size_d // dec, dec, step_keys)
            one = one + seen[:, j * step_keys:(j + 1) * step_keys][None]
            kept.append(one.reshape(size_d, step_keys))
            held.append(keys)
        top = functools.reduce(jnp.maximum, [jnp.max(x, axis=1, keepdims=True) for x in kept]) * exponent
        weight, mixed = 0.0, 0.0
        for x, keys in zip(kept, held):
            raised = jnp.exp2(x * exponent - top)
            weight += jnp.sum(raised, axis=1, keepdims=True)
            mixed += jnp.dot(raised.astype(BF16), keys[:, :latent], preferred_element_type=F32)
        mixed_d[at, :] = (mixed / weight).astype(BF16)
        return carry

    lax.fori_loop(0, 2, decode_block, 0)
    share_on(*gang_a)

    def give(device):
        source = values_out.at[pl.ds(pl.multiple_of(place_of(jnp.int32(device)), 4), q_rows)]
        dest = out_ref.at[:, pl.ds(pl.multiple_of(hd * heads, heads), heads), :]

        @pl.when(hd != device)
        def _():
            pltpu.make_async_remote_copy(
                src_ref=source, dst_ref=dest, send_sem=out_send, recv_sem=out_recv,
                device_id=(me, device), device_id_type=MESH,
            ).start()

        @pl.when(hd == device)
        def _():
            pltpu.make_async_copy(source, dest, own_sem.at[5]).start()

    def put_values(first, count, mixed, base):
        for h in range(heads):
            values[pl.ds(first * heads + h, count, stride=heads), :] = jnp.dot(
                mixed[pl.ds(base + h * count, count), :], value_up[h], preferred_element_type=F32
            )
        done = values[pl.ds(first * heads, count * heads), :].astype(BF16)
        values_out[pl.ds(first, count)] = done.reshape(count, heads, done.shape[1])

    loads[5].wait()
    put_values(pre, dec, mixed_d, 0)
    give(nh - 1)

    share_end(*gang_a)
    own_rows[1].wait()
    wait_bytes(in1.at[pl.ds(0, nd - 1)], recv1)
    target = spread_rows(late, part)
    keys_b[hd] = (
        pick_rows(target, 0.0, in0[...].reshape(nd * part, width))
        + pick_rows(target, float(nd * part), in1[...].reshape(nd * part, width))
    ).astype(BF16)
    share_own(*gang_b)

    size = heads * part_rows // 2
    key_count = reqs // 2 * block_rows

    def early_block(index, carry):
        at = pl.ds(pl.multiple_of(index * size, size), size)
        query = query_p[at, :]
        local = latents[:pre, :]
        keys = keys_a[...].reshape(key_count, width)
        row = lax.rem(iota((size, pre), 0), part_rows) + (index // 2) * part_rows
        group = row // q_rows
        moved = jnp.where(group < front, 2 * group, 2 * (group - front) + 1) - group
        row = jnp.where(group < 2 * front, row + moved * q_rows, row)
        second = jnp.where(iota((size, pre), 1) <= row, scores(query, local), HIDDEN)
        first = scores(query, keys)
        top = jnp.maximum(
            jnp.max(first, axis=1, keepdims=True), jnp.max(second, axis=1, keepdims=True)
        ) * exponent
        raised1 = jnp.exp2(first * exponent - top)
        raised2 = jnp.exp2(second * exponent - top)
        weight = jnp.sum(raised1, axis=1, keepdims=True) + jnp.sum(raised2, axis=1, keepdims=True)
        mixed = jnp.dot(raised1.astype(BF16), keys[:, :latent], preferred_element_type=F32)
        mixed += jnp.dot(raised2.astype(BF16), local[:, :latent], preferred_element_type=F32)
        acc[at, :] = mixed
        peak[at, :] = jnp.broadcast_to(top, (size, 128))
        total[at, :] = jnp.broadcast_to(weight, (size, 128))
        return carry

    def late_block(index, carry):
        at = pl.ds(pl.multiple_of(index * size, size), size)
        keys = keys_b[...].reshape(key_count, width)
        first = scores(query_p[at, :], keys)
        old = peak[at, :][:, 0:1]
        top = jnp.maximum(old, jnp.max(first, axis=1, keepdims=True) * exponent)
        fix = jnp.exp2(old - top)
        raised = jnp.exp2(first * exponent - top)
        weight = total[at, :][:, 0:1] * fix + jnp.sum(raised, axis=1, keepdims=True)
        mixed = acc[at, :] * fix
        mixed += jnp.dot(raised.astype(BF16), keys[:, :latent], preferred_element_type=F32)
        mixed_p[at, :] = (mixed / weight).astype(BF16)
        return carry

    lax.fori_loop(0, 2, early_block, 0)
    share_on(*gang_b)
    lax.fori_loop(2, 4, early_block, 0)
    share_end(*gang_b)
    lax.fori_loop(0, 2, late_block, 0)
    put_values(0, part_rows, mixed_p, 0)
    for device in range(0, 2 * front, 2):
        give(device)
    lax.fori_loop(2, 4, late_block, 0)
    put_values(part_rows, part_rows, mixed_p, heads * part_rows)
    for device in [*range(1, 2 * front, 2), *range(2 * front, nh - 1)]:
        give(device)

    share_sent(*gang_a)
    share_sent(*gang_b)
    wait_bytes(nope_in.at[pl.ds(0, rows - q_rows)], nope_send)
    wait_bytes(rope_in.at[pl.ds(0, nh - 1)], rope_send)
    wait_bytes(in0.at[pl.ds(0, nd - 1)], send0)
    wait_bytes(in1.at[pl.ds(0, nd - 1)], send1)
    wait_bytes(table.at[pl.ds(0, nd - 1)], id_send)
    wait_bytes(values_out.at[pl.ds(0, q_rows)], own_sem.at[5])
    wait_bytes(values_out.at[pl.ds(0, rows - q_rows)], out_send)
    wait_bytes(values_out.at[pl.ds(0, rows - q_rows)], out_recv)


def body(
    queries, latents, cache_pool, key_up, value_up, prefix_rank, prefix_block, decode_start, decode_length
):
    nd, nh = lax.axis_size("dp"), lax.axis_size("head")
    q_rows, all_heads, q_width = queries.shape
    heads, nope_dim, latent = key_up.shape
    rows = q_rows * nh
    blocks, block_rows, width = cache_pool.shape
    part = block_rows // nh
    pair = CAP * part
    reqs = prefix_block.shape[0]
    dec = decode_start.shape[0]
    pre = rows - dec
    v_dim = value_up.shape[2]
    anywhere = pl.BlockSpec(memory_space=pl.ANY)
    vmem = pl.BlockSpec(memory_space=pltpu.VMEM)
    dma = pltpu.SemaphoreType.DMA
    half_keys = (nh, reqs // 2 * part, width)
    half_heads = heads // 2
    buffers = [
        ((q_rows, q_width, all_heads), BF16),
        (latents.shape, BF16),
        (cache_pool.shape, BF16),
        (key_up.shape, BF16),
        (value_up.shape, BF16),
        ((blocks, pair, width), BF16),
        ((nd, 1, 128), F32),
        ((nd, 1, 128), F32),
        ((q_rows, all_heads, nope_dim), BF16),
        ((nh, q_rows * half_heads, 2 * (q_width - nope_dim)), BF16),
        ((rows, heads, nope_dim), BF16),
        ((nh, q_rows * half_heads, 2 * (q_width - nope_dim)), BF16),
        ((rows * heads, nope_dim), F32),
        ((rows * half_heads, 2 * (q_width - nope_dim)), F32),
        ((nd, part, width), BF16),
        ((nd, part, width), BF16),
        ((nd, part, width), BF16),
        ((nd, part, width), BF16),
        (half_keys, BF16),
        (half_keys, BF16),
        ((pre * heads, width), BF16),
        ((dec * heads, width), BF16),
        ((pre * heads, latent), BF16),
        ((dec * heads, latent), BF16),
        ((rows * heads, v_dim), F32),
        ((rows, heads, v_dim), BF16),
        ((dec, blocks * block_rows), F32),
        ((pre * heads, latent), F32),
        ((pre * heads, 128), F32),
        ((pre * heads, 128), F32),
    ]
    return pl.pallas_call(
        kernel,
        out_shape=jax.ShapeDtypeStruct((q_rows, all_heads, v_dim), BF16),
        in_specs=[anywhere] * 5 + [vmem] * 4,
        out_specs=anywhere,
        scratch_shapes=[pltpu.VMEM(shape, dtype) for shape, dtype in buffers]
        + [dma((6,))] + [dma] * 10 + [dma((nh,))] * 4 + [dma, dma, dma((6,))],
        compiler_params=pltpu.CompilerParams(
            collective_id=0, has_side_effects=True, vmem_limit_bytes=60 * 2**20
        ),
        name="serve",
    )(
        jnp.swapaxes(queries, 1, 2), latents, cache_pool, key_up, value_up,
        prefix_rank.reshape(1, reqs), prefix_block.reshape(1, reqs),
        decode_start.reshape(1, dec), decode_length.reshape(1, dec),
    )


def solution(mesh):
    return jax.shard_map(
        body,
        mesh=mesh,
        in_specs=(
            P(("dp", "head"), None, None),
            P("dp", None),
            P("dp", None, None),
            P("head", None, None),
            P("head", None, None),
            P("dp", None),
            P("dp"),
            P("dp"),
            P("dp"),
        ),
        out_specs=P(("dp", "head"), None, None),
        check_vma=False,
    )
```

```python
import functools
import math

import jax
import jax.numpy as jnp
from jax import lax
from jax.experimental import pallas as pl
from jax.experimental.pallas import tpu as pltpu
from jax.sharding import PartitionSpec as P

MESH = pl.DeviceIdType.MESH
CAP = 2
F32 = jnp.float32
BF16 = jnp.bfloat16
HIDDEN = -1e30


def iota(shape, dim):
    return lax.broadcasted_iota(jnp.int32, shape, dim)


def wait_bytes(ref, sem):
    pltpu.make_async_copy(ref, ref, sem).wait()


def gather_lists(rank_row, block_row, nd):
    reqs = rank_row.shape[1]
    half = reqs // 2
    row_i, col_i = iota((reqs, reqs), 0), iota((reqs, reqs), 1)

    def down(mask, values=1.0):
        return jnp.sum(jnp.where(mask, values, 0.0), axis=0, keepdims=True)

    def across(mask, values=1.0):
        return jnp.sum(jnp.where(mask, values, 0.0), axis=1, keepdims=True)

    rank_col = across(row_i == col_i, rank_row)
    same = rank_col == rank_row
    slot_row = down(same & (row_i < col_i))
    slot_col = across(same & (col_i < row_i))
    hit = rank_row == iota((nd, reqs), 0).astype(F32)
    want0 = across(hit & (slot_row == 0.0), block_row + 1.0) - 1.0
    want1 = across(hit & (slot_row == 1.0), block_row + 1.0) - 1.0
    spot_row = down((row_i < col_i) & (slot_col == 0.0))
    spot_col = across((col_i < row_i) & (slot_row == 0.0))
    early_row = (slot_row == 0.0) & (spot_row < half)
    early_col = (slot_col == 0.0) & (spot_col < half)
    late_row = down((row_i < col_i) & jnp.logical_not(early_col))
    order = iota((half, reqs), 0).astype(F32)
    early = across((order == spot_row) & early_row, rank_row)
    late = across((order == late_row) & jnp.logical_not(early_row), slot_row * nd + rank_row)
    return want0, want1, early, late


def spread_rows(column, part):
    count = column.shape[0]
    expand = (iota((count * part, count), 0) // part == iota((count * part, count), 1)).astype(BF16)
    wide = jnp.broadcast_to(column, (count, 128)).astype(BF16)
    spread = jnp.dot(expand, wide, preferred_element_type=F32)[:, 0:1]
    return spread * part + lax.rem(iota((count * part, 1), 0), part).astype(F32)


def pick_rows(target, first, source):
    total = source.shape[0]
    pick = (iota((target.shape[0], total), 1).astype(F32) + first == target).astype(BF16)
    return jnp.dot(pick, source, preferred_element_type=F32)


def scores(query, keys):
    return lax.dot_general(query, keys, (((1,), (1,)), ((), ())), preferred_element_type=F32)


def kernel(
    q_ref, latents_hbm, cache_hbm, key_up_hbm, value_up_hbm, rank_ref, block_ref, start_ref, length_ref,
    out_ref,
    q_in, latents, cache, key_up, value_up, rows_here, table, ids,
    nope_out, rope_out, nope_in, rope_in, nope, rope, out0, out1, in0, in1, keys_a, keys_b,
    query_p, query_d, mixed_p, mixed_d, values, values_out, seen, acc, peak, total, causal,
    local_sem, id_send, id_recv, nope_send, nope_recv, rope_send, rope_recv,
    send0, recv0, send1, recv1, a_send, a_recv, b_send, b_recv, out_send, out_recv, own_sem,
):
    nd, nh = lax.axis_size("dp"), lax.axis_size("head")
    chips = nh // 2
    me, hd = lax.axis_index("dp"), lax.axis_index("head")
    chip, core = hd // 2, hd % 2
    sibling = chip * 2 + 1 - core
    blocks, block_rows, width = cache_hbm.shape
    part = block_rows // nh
    pair = CAP * part
    q_rows, q_width, all_heads = q_ref.shape
    heads, nope_dim, latent = key_up_hbm.shape
    rope_dim = q_width - nope_dim
    rows = q_rows * nh
    reqs = rank_ref.shape[1]
    dec = start_ref.shape[1]
    pre = rows - dec
    pool = blocks * block_rows
    exponent = float(q_width) ** (-0.5) * math.log2(math.e)
    front = chips - 1

    def place_of(device):
        moved = jnp.where(device % 2 == 0, device // 2, front + device // 2)
        return jnp.where(device < 2 * front, moved, device) * q_rows

    loads = [
        pltpu.make_async_copy(source, dest, local_sem.at[i])
        for i, (source, dest) in enumerate([
            (q_ref, q_in),
            (cache_hbm.at[:, pl.ds(pl.multiple_of(chip * pair, pair), pair), :], rows_here),
            (key_up_hbm, key_up), (latents_hbm, latents), (cache_hbm, cache), (value_up_hbm, value_up),
        ])
    ]
    for load in loads:
        load.start()
    barrier = pltpu.get_barrier_semaphore()

    def greet_dp(step, carry):
        pl.semaphore_signal(barrier, inc=1, device_id=(lax.rem(me + step, nd), hd), device_id_type=MESH)
        return carry

    def greet_head(step, carry):
        pl.semaphore_signal(barrier, inc=1, device_id=(me, lax.rem(hd + step, nh)), device_id_type=MESH)
        return carry

    lax.fori_loop(1, nd, greet_dp, 0)
    lax.fori_loop(1, nh, greet_head, 0)

    want0, want1, early, late = gather_lists(
        rank_ref[...].astype(F32), block_ref[...].astype(F32), nd
    )
    lane = iota((nd, 128), 1)
    table[:, 0, :] = jnp.where(lane == 0, want0, jnp.where(lane == 1, want1, 0.0))

    loads[0].wait()
    half_heads = heads // 2

    def turn(step, carry):
        turned = []
        for k in range(2):
            one = jnp.transpose(q_in[2 * step + k].astype(F32), (1, 0))
            nope_out[2 * step + k] = one[:, :nope_dim].astype(BF16)
            both = one[:, nope_dim:].reshape(nh, 2, half_heads, rope_dim)
            turned.append(jnp.concatenate([both[:, 0], both[:, 1]], axis=2))
        at = pl.ds(pl.multiple_of(step * 2 * half_heads, 2 * half_heads), 2 * half_heads)
        rope_out[:, at, :] = jnp.concatenate(turned, axis=1).astype(BF16)
        return carry

    lax.fori_loop(0, q_rows // 2, turn, 0)

    pre_row = iota((pre, 1), 0)
    group = pre_row // q_rows
    moved = jnp.where(group < front, 2 * group, 2 * (group - front) + 1) - group
    pre_row = jnp.where(group < 2 * front, pre_row + moved * q_rows, pre_row)
    causal[...] = jnp.where(iota((pre, pre), 1) <= pre_row, 0.0, HIDDEN)

    pl.semaphore_wait(barrier, nd - 1 + nh - 1)

    def send_ids(step, carry):
        peer = lax.rem(me + step, nd)
        pltpu.make_async_remote_copy(
            src_ref=table.at[peer], dst_ref=ids.at[me], send_sem=id_send, recv_sem=id_recv,
            device_id=(peer, hd), device_id_type=MESH,
        ).start()
        return carry

    lax.fori_loop(1, nd, send_ids, 0)
    own_ids = pltpu.make_async_copy(table.at[me], ids.at[me], own_sem.at[0])
    own_ids.start()

    here = place_of(hd)

    def q_copies(peer, remote):
        nope_from = nope_out.at[:, pl.ds(pl.multiple_of(peer * heads, heads), heads), :]
        nope_to = nope_in.at[pl.ds(here, q_rows)]
        rope_to = rope_in.at[here // q_rows]
        if not remote:
            return [
                pltpu.make_async_copy(nope_from, nope_to, own_sem.at[1]),
                pltpu.make_async_copy(rope_out.at[peer], rope_to, own_sem.at[2]),
            ]
        return [
            pltpu.make_async_remote_copy(
                src_ref=nope_from, dst_ref=nope_to, send_sem=nope_send, recv_sem=nope_recv,
                device_id=(me, peer), device_id_type=MESH,
            ),
            pltpu.make_async_remote_copy(
                src_ref=rope_out.at[peer], dst_ref=rope_to, send_sem=rope_send, recv_sem=rope_recv,
                device_id=(me, peer), device_id_type=MESH,
            ),
        ]

    def send_q(step, carry):
        for copy in q_copies(lax.rem(hd + step, nh), True):
            copy.start()
        return carry

    lax.fori_loop(1, nh, send_q, 0)
    own_q = q_copies(hd, False)
    for copy in own_q:
        copy.start()

    loads[1].wait()
    own_ids.wait()
    wait_bytes(ids.at[pl.ds(0, nd - 1)], id_recv)
    expand = (iota((nd * part, nd), 0) // part == iota((nd * part, nd), 1)).astype(BF16)
    asked = jnp.dot(expand, ids[:, 0, :].astype(BF16), preferred_element_type=F32)
    offset = (lax.rem(iota((nd * part, 1), 0), part) + core * part).astype(F32)

    def row_copy(source, dest, send_sem, recv_sem, peer):
        return pltpu.make_async_remote_copy(
            src_ref=source.at[peer], dst_ref=dest.at[me], send_sem=send_sem, recv_sem=recv_sem,
            device_id=(peer, hd), device_id_type=MESH,
        )

    own_rows = []
    for slot, (source, dest, send_sem, recv_sem) in enumerate(
        [(out0, in0, send0, recv0), (out1, in1, send1, recv1)]
    ):
        wanted = asked[:, slot:slot + 1]
        target = jnp.where(wanted < 0.0, -1e6, wanted * pair) + offset
        picked = pick_rows(target, 0.0, rows_here[...].reshape(blocks * pair, width))
        source[...] = picked.astype(BF16).reshape(nd, part, width)

        def send_rows(step, carry, source=source, dest=dest, send_sem=send_sem, recv_sem=recv_sem):
            row_copy(source, dest, send_sem, recv_sem, lax.rem(me + step, nd)).start()
            return carry

        if slot == 0: lax.fori_loop(1, nd, send_rows, 0)
        own = pltpu.make_async_copy(source.at[me], dest.at[me], own_sem.at[3 + slot])
        own.start()
        own_rows.append(own)

    wait_bytes(in0.at[pl.ds(0, nd - 1)], send0)
    lax.fori_loop(1, nd, send_rows, 0)
    for copy in own_q:
        copy.wait()
    loads[2].wait()
    wait_bytes(nope_in.at[pl.ds(0, rows - q_rows)], nope_recv)
    wait_bytes(rope_in.at[pl.ds(0, nh - 1)], rope_recv)
    nope[...] = nope_in[...].reshape(rows * heads, nope_dim).astype(F32)
    rope[...] = rope_in[...].reshape(rows * half_heads, 2 * rope_dim).astype(F32)
    part_rows = pre // 2

    def put_query(h, columns, value):
        for side in range(2):
            at = pl.ds((side * heads + h) * part_rows, part_rows)
            query_p[at, columns] = value[side * part_rows:(side + 1) * part_rows]
        query_d[pl.ds(h * dec, dec), columns] = value[pre:]

    for h in range(heads):
        picked = nope[pl.ds(h, rows, stride=heads), :].astype(BF16)
        absorbed = jnp.dot(picked, key_up[h], preferred_element_type=F32).astype(BF16)
        put_query(h, slice(0, latent), absorbed)
    for h in range(half_heads):
        both = rope[pl.ds(h, rows, stride=half_heads), :].astype(BF16)
        put_query(h, slice(latent, width), both[:, :rope_dim])
        put_query(h + half_heads, slice(latent, width), both[:, rope_dim:])

    def share(keys, send_sem, recv_sem, index, peer, slot):
        return pltpu.make_async_remote_copy(
            src_ref=keys.at[index], dst_ref=keys.at[index], send_sem=send_sem.at[slot],
            recv_sem=recv_sem.at[index], device_id=(me, peer), device_id_type=MESH,
        )

    def share_own(*gang):
        for step in range(1, chips):
            share(*gang, hd, lax.rem(hd + 2 * step, nh), step).start()
        share(*gang, hd, sibling, 0).start()

    def share_on(*gang):
        for step in range(1, chips):
            source = lax.rem(hd - 2 * step + nh, nh)
            share(*gang, source, sibling, 0).wait_recv()
            share(*gang, source, sibling, chips + step).start()

    def share_end(*gang):
        for step in range(chips):
            share(*gang, lax.rem(sibling + 2 * step, nh), sibling, 0).wait_recv()

    def share_sent(*gang):
        for slot in [*range(chips), *range(chips + 1, 2 * chips)]:
            share(*gang, hd, sibling, slot).wait_send()

    gang_a = (keys_a, a_send, a_recv)
    gang_b = (keys_b, b_send, b_recv)

    def give(device):
        source = values_out.at[pl.ds(pl.multiple_of(place_of(jnp.int32(device)), 4), q_rows)]
        dest = out_ref.at[:, pl.ds(pl.multiple_of(hd * heads, heads), heads), :]

        @pl.when(hd != device)
        def _():
            pltpu.make_async_remote_copy(
                src_ref=source, dst_ref=dest, send_sem=out_send, recv_sem=out_recv,
                device_id=(me, device), device_id_type=MESH,
            ).start()

        @pl.when(hd == device)
        def _():
            pltpu.make_async_copy(source, dest, own_sem.at[5]).start()

    def put_values(first, count, mixed, base):
        for h in range(heads):
            values[pl.ds(first * heads + h, count, stride=heads), :] = jnp.dot(
                mixed[pl.ds(base + h * count, count), :], value_up[h], preferred_element_type=F32
            )
        done = values[pl.ds(first * heads, count * heads), :].astype(BF16)
        values_out[pl.ds(first, count)] = done.reshape(count, heads, done.shape[1])

    own_rows[0].wait()
    wait_bytes(in0.at[pl.ds(0, nd - 1)], recv0)
    first_rows = in0[...].reshape(nd * part, width)
    keys_a[hd] = pick_rows(spread_rows(early, part), 0.0, first_rows).astype(BF16)
    share_own(*gang_a)

    loads[3].wait()
    loads[4].wait()
    eye = iota((dec, dec), 0) == iota((dec, dec), 1)
    start = jnp.sum(jnp.where(eye, start_ref[...].astype(F32), 0.0), axis=1, keepdims=True)
    length = jnp.sum(jnp.where(eye, length_ref[...].astype(F32), 0.0), axis=1, keepdims=True)
    place = iota((dec, pool), 1).astype(F32) - start
    seen[...] = jnp.where((place >= 0.0) & (place < length), 0.0, HIDDEN)
    step_blocks = blocks // 4
    step_keys = step_blocks * block_rows
    size_d = heads * dec

    def decode_block(index, carry):
        at = pl.ds(pl.multiple_of(index * size_d, size_d), size_d)
        query = query_d[at, :]
        local = latents[rows - pre:, :]
        own = lax.rem(iota((size_d, pre), 0), dec) + (pre - dec)
        kept = [jnp.where(iota((size_d, pre), 1) == own, scores(query, local), HIDDEN)]
        held = [local]
        for j in range(4):
            keys = cache[j * step_blocks:(j + 1) * step_blocks].reshape(step_keys, width)
            one = scores(query, keys).reshape(size_d // dec, dec, step_keys)
            one = one + seen[:, j * step_keys:(j + 1) * step_keys][None]
            kept.append(one.reshape(size_d, step_keys))
            held.append(keys)
        top = functools.reduce(jnp.maximum, [jnp.max(x, axis=1, keepdims=True) for x in kept]) * exponent
        weight, mixed = 0.0, 0.0
        for x, keys in zip(kept, held):
            raised = jnp.exp2(x * exponent - top)
            weight += jnp.sum(raised, axis=1, keepdims=True)
            mixed += jnp.dot(raised.astype(BF16), keys[:, :latent], preferred_element_type=F32)
        mixed_d[at, :] = (mixed / weight).astype(BF16)
        return carry

    decode_block(0, 0)
    loads[5].wait()
    put_values(pre, dec, mixed_d, 0)
    give(nh - 1)

    share_on(*gang_a)

    own_rows[1].wait()
    wait_bytes(in1.at[pl.ds(0, nd - 1)], recv1)
    target = spread_rows(late, part)
    keys_b[hd] = (
        pick_rows(target, 0.0, in0[...].reshape(nd * part, width))
        + pick_rows(target, float(nd * part), in1[...].reshape(nd * part, width))
    ).astype(BF16)
    share_own(*gang_b)

    share_end(*gang_a)

    size = heads * part_rows // 2

    pieces = 2
    piece = nh // pieces

    def soften(kept, held, top):
        weight, mixed = 0.0, 0.0
        for x, keys in zip(kept, held):
            raised = jnp.exp2(x * exponent - top)
            weight += jnp.sum(raised, axis=1, keepdims=True)
            mixed += jnp.dot(raised.astype(BF16), keys[:, :latent], preferred_element_type=F32)
        return weight, mixed

    def highest(kept):
        return functools.reduce(jnp.maximum, [jnp.max(x, axis=1, keepdims=True) for x in kept]) * exponent

    def early_block(index, carry):
        at = pl.ds(pl.multiple_of(index * size, size), size)
        query = query_p[at, :]
        side = pl.ds(pl.multiple_of(index // 2 * part_rows, part_rows), part_rows)
        held = [keys_a[j * piece:(j + 1) * piece].reshape(-1, width) for j in range(pieces)]
        kept = [scores(query, keys) for keys in held]
        held.append(latents[:pre, :])
        own = scores(query, held[-1]).reshape(size // part_rows, part_rows, pre) + causal[side, :][None]
        kept.append(own.reshape(size, pre))
        top = highest(kept)
        weight, mixed = soften(kept, held, top)
        acc[at, :] = mixed
        peak[at, :] = jnp.broadcast_to(top, (size, 128))
        total[at, :] = jnp.broadcast_to(weight, (size, 128))
        return carry

    def late_block(index, carry):
        at = pl.ds(pl.multiple_of(index * size, size), size)
        query = query_p[at, :]
        held = [keys_b[j * piece:(j + 1) * piece].reshape(-1, width) for j in range(pieces)]
        kept = [scores(query, keys) for keys in held]
        old = peak[at, :][:, 0:1]
        top = jnp.maximum(old, highest(kept))
        fix = jnp.exp2(old - top)
        weight, mixed = soften(kept, held, top)
        weight += total[at, :][:, 0:1] * fix
        mixed_p[at, :] = ((acc[at, :] * fix + mixed) / weight).astype(BF16)
        return carry

    lax.fori_loop(0, 2, early_block, 0, unroll=True)
    share_on(*gang_b)
    lax.fori_loop(2, 4, early_block, 0, unroll=True)
    share_end(*gang_b)
    lax.fori_loop(0, 2, late_block, 0, unroll=True)
    put_values(0, part_rows, mixed_p, 0)
    for device in range(0, 2 * front, 2):
        give(device)
    lax.fori_loop(2, 4, late_block, 0, unroll=True)
    put_values(part_rows, part_rows, mixed_p, heads * part_rows)
    for device in [*range(1, 2 * front, 2), *range(2 * front, nh - 1)]:
        give(device)

    share_sent(*gang_a)
    share_sent(*gang_b)
    wait_bytes(nope_in.at[pl.ds(0, rows - q_rows)], nope_send)
    wait_bytes(rope_in.at[pl.ds(0, nh - 1)], rope_send)
    wait_bytes(in1.at[pl.ds(0, nd - 1)], send1)
    wait_bytes(table.at[pl.ds(0, nd - 1)], id_send)
    wait_bytes(values_out.at[pl.ds(0, q_rows)], own_sem.at[5])
    wait_bytes(values_out.at[pl.ds(0, rows - q_rows)], out_send)
    wait_bytes(values_out.at[pl.ds(0, rows - q_rows)], out_recv)


def body(
    queries, latents, cache_pool, key_up, value_up, prefix_rank, prefix_block, decode_start, decode_length
):
    nd, nh = lax.axis_size("dp"), lax.axis_size("head")
    q_rows, all_heads, q_width = queries.shape
    heads, nope_dim, latent = key_up.shape
    rows = q_rows * nh
    blocks, block_rows, width = cache_pool.shape
    part = block_rows // nh
    pair = CAP * part
    reqs = prefix_block.shape[0]
    dec = decode_start.shape[0]
    pre = rows - dec
    v_dim = value_up.shape[2]
    anywhere = pl.BlockSpec(memory_space=pl.ANY)
    vmem = pl.BlockSpec(memory_space=pltpu.VMEM)
    dma = pltpu.SemaphoreType.DMA
    half_keys = (nh, reqs // 2 * part, width)
    half_heads = heads // 2
    buffers = [
        ((q_rows, q_width, all_heads), BF16),
        (latents.shape, BF16),
        (cache_pool.shape, BF16),
        (key_up.shape, BF16),
        (value_up.shape, BF16),
        ((blocks, pair, width), BF16),
        ((nd, 1, 128), F32),
        ((nd, 1, 128), F32),
        ((q_rows, all_heads, nope_dim), BF16),
        ((nh, q_rows * half_heads, 2 * (q_width - nope_dim)), BF16),
        ((rows, heads, nope_dim), BF16),
        ((nh, q_rows * half_heads, 2 * (q_width - nope_dim)), BF16),
        ((rows * heads, nope_dim), F32),
        ((rows * half_heads, 2 * (q_width - nope_dim)), F32),
        ((nd, part, width), BF16),
        ((nd, part, width), BF16),
        ((nd, part, width), BF16),
        ((nd, part, width), BF16),
        (half_keys, BF16),
        (half_keys, BF16),
        ((pre * heads, width), BF16),
        ((dec * heads, width), BF16),
        ((pre * heads, latent), BF16),
        ((dec * heads, latent), BF16),
        ((rows * heads, v_dim), F32),
        ((rows, heads, v_dim), BF16),
        ((dec, blocks * block_rows), F32),
        ((pre * heads, latent), F32),
        ((pre * heads, 128), F32),
        ((pre * heads, 128), F32),
        ((pre, pre), F32),
    ]
    return pl.pallas_call(
        kernel,
        out_shape=jax.ShapeDtypeStruct((q_rows, all_heads, v_dim), BF16),
        in_specs=[anywhere] * 5 + [vmem] * 4,
        out_specs=anywhere,
        scratch_shapes=[pltpu.VMEM(shape, dtype) for shape, dtype in buffers]
        + [dma((6,))] + [dma] * 10 + [dma((nh,))] * 4 + [dma, dma, dma((6,))],
        compiler_params=pltpu.CompilerParams(
            collective_id=0, has_side_effects=True, vmem_limit_bytes=60 * 2**20
        ),
        name="serve",
    )(
        jnp.swapaxes(queries, 1, 2), latents, cache_pool, key_up, value_up,
        prefix_rank.reshape(1, reqs), prefix_block.reshape(1, reqs),
        decode_start.reshape(1, dec), decode_length.reshape(1, dec),
    )


def solution(mesh):
    return jax.shard_map(
        body,
        mesh=mesh,
        in_specs=(
            P(("dp", "head"), None, None),
            P("dp", None),
            P("dp", None, None),
            P("head", None, None),
            P("head", None, None),
            P("dp", None),
            P("dp"),
            P("dp"),
            P("dp"),
        ),
        out_specs=P(("dp", "head"), None, None),
        check_vma=False,
    )
```

```python
import functools
import math

import jax
import jax.numpy as jnp
from jax import lax
from jax.experimental import pallas as pl
from jax.experimental.pallas import tpu as pltpu
from jax.sharding import PartitionSpec as P

MESH = pl.DeviceIdType.MESH
CAP = 2
F32 = jnp.float32
BF16 = jnp.bfloat16
HIDDEN = -1e30


def iota(shape, dim):
    return lax.broadcasted_iota(jnp.int32, shape, dim)


def wait_bytes(ref, sem):
    pltpu.make_async_copy(ref, ref, sem).wait()


def gather_lists(rank_row, block_row, nd):
    reqs = rank_row.shape[1]
    half = reqs // 2
    row_i, col_i = iota((reqs, reqs), 0), iota((reqs, reqs), 1)

    def down(mask, values=1.0):
        return jnp.sum(jnp.where(mask, values, 0.0), axis=0, keepdims=True)

    def across(mask, values=1.0):
        return jnp.sum(jnp.where(mask, values, 0.0), axis=1, keepdims=True)

    rank_col = across(row_i == col_i, rank_row)
    same = rank_col == rank_row
    slot_row = down(same & (row_i < col_i))
    slot_col = across(same & (col_i < row_i))
    hit = rank_row == iota((nd, reqs), 0).astype(F32)
    want0 = across(hit & (slot_row == 0.0), block_row + 1.0) - 1.0
    want1 = across(hit & (slot_row == 1.0), block_row + 1.0) - 1.0
    spot_row = down((row_i < col_i) & (slot_col == 0.0))
    spot_col = across((col_i < row_i) & (slot_row == 0.0))
    early_row = (slot_row == 0.0) & (spot_row < half)
    early_col = (slot_col == 0.0) & (spot_col < half)
    late_row = down((row_i < col_i) & jnp.logical_not(early_col))
    order = iota((half, reqs), 0).astype(F32)
    early = across((order == spot_row) & early_row, rank_row)
    late = across((order == late_row) & jnp.logical_not(early_row), slot_row * nd + rank_row)
    return want0, want1, early, late


def spread_rows(column, part):
    count = column.shape[0]
    expand = (iota((count * part, count), 0) // part == iota((count * part, count), 1)).astype(BF16)
    wide = jnp.broadcast_to(column, (count, 128)).astype(BF16)
    spread = jnp.dot(expand, wide, preferred_element_type=F32)[:, 0:1]
    return spread * part + lax.rem(iota((count * part, 1), 0), part).astype(F32)


def pick_rows(target, first, source):
    total = source.shape[0]
    pick = (iota((target.shape[0], total), 1).astype(F32) + first == target).astype(BF16)
    return jnp.dot(pick, source, preferred_element_type=F32)


def scores(query, keys):
    return lax.dot_general(query, keys, (((1,), (1,)), ((), ())), preferred_element_type=F32)


def kernel(
    q_ref, latents_hbm, cache_hbm, key_up_hbm, value_up_hbm, rank_ref, block_ref, start_ref, length_ref,
    out_ref,
    q_in, latents, cache, key_up, value_up, rows_here, table, ids,
    nope_out, rope_out, nope_in, rope_in, nope, rope, out0, out1, in0, in1, keys_a, keys_b,
    query_p, query_d, mixed_p, mixed_d, values, values_out, seen, acc, peak, total, causal,
    local_sem, id_send, id_recv, nope_send, nope_recv, rope_send, rope_recv,
    send0, recv0, send1, recv1, a_send, a_recv, b_send, b_recv, out_send, out_recv, own_sem,
):
    nd, nh = lax.axis_size("dp"), lax.axis_size("head")
    chips = nh // 2
    me, hd = lax.axis_index("dp"), lax.axis_index("head")
    chip, core = hd // 2, hd % 2
    sibling = chip * 2 + 1 - core
    blocks, block_rows, width = cache_hbm.shape
    part = block_rows // nh
    pair = CAP * part
    q_rows, q_width, all_heads = q_ref.shape
    heads, nope_dim, latent = key_up_hbm.shape
    rope_dim = q_width - nope_dim
    rows = q_rows * nh
    reqs = rank_ref.shape[1]
    dec = start_ref.shape[1]
    pre = rows - dec
    pool = blocks * block_rows
    exponent = float(q_width) ** (-0.5) * math.log2(math.e)
    front = chips - 1

    def place_of(device):
        moved = jnp.where(device % 2 == 0, device // 2, front + device // 2)
        return jnp.where(device < 2 * front, moved, device) * q_rows

    loads = [
        pltpu.make_async_copy(source, dest, local_sem.at[i])
        for i, (source, dest) in enumerate([
            (q_ref, q_in),
            (cache_hbm.at[:, pl.ds(pl.multiple_of(chip * pair, pair), pair), :], rows_here),
            (key_up_hbm, key_up), (latents_hbm, latents), (cache_hbm, cache), (value_up_hbm, value_up),
        ])
    ]
    for load in loads:
        load.start()
    barrier = pltpu.get_barrier_semaphore()

    def greet_dp(step, carry):
        pl.semaphore_signal(barrier, inc=1, device_id=(lax.rem(me + step, nd), hd), device_id_type=MESH)
        return carry

    def greet_head(step, carry):
        pl.semaphore_signal(barrier, inc=1, device_id=(me, lax.rem(hd + step, nh)), device_id_type=MESH)
        return carry

    lax.fori_loop(1, nd, greet_dp, 0)
    lax.fori_loop(1, nh, greet_head, 0)

    want0, want1, early, late = gather_lists(
        rank_ref[...].astype(F32), block_ref[...].astype(F32), nd
    )
    lane = iota((nd, 128), 1)
    table[:, 0, :] = jnp.where(lane == 0, want0, jnp.where(lane == 1, want1, 0.0))

    loads[0].wait()
    half_heads = heads // 2

    def turn(step, carry):
        turned = []
        for k in range(2):
            one = jnp.transpose(q_in[2 * step + k].astype(F32), (1, 0))
            nope_out[2 * step + k] = one[:, :nope_dim].astype(BF16)
            both = one[:, nope_dim:].reshape(nh, 2, half_heads, rope_dim)
            turned.append(jnp.concatenate([both[:, 0], both[:, 1]], axis=2))
        at = pl.ds(pl.multiple_of(step * 2 * half_heads, 2 * half_heads), 2 * half_heads)
        rope_out[:, at, :] = jnp.concatenate(turned, axis=1).astype(BF16)
        return carry

    lax.fori_loop(0, q_rows // 2, turn, 0)

    pre_row = iota((pre, 1), 0)
    group = pre_row // q_rows
    moved = jnp.where(group < front, 2 * group, 2 * (group - front) + 1) - group
    pre_row = jnp.where(group < 2 * front, pre_row + moved * q_rows, pre_row)
    causal[...] = jnp.where(iota((pre, pre), 1) <= pre_row, 0.0, HIDDEN)

    pl.semaphore_wait(barrier, nd - 1 + nh - 1)

    def send_ids(step, carry):
        peer = lax.rem(me + step, nd)
        pltpu.make_async_remote_copy(
            src_ref=table.at[peer], dst_ref=ids.at[me], send_sem=id_send, recv_sem=id_recv,
            device_id=(peer, hd), device_id_type=MESH,
        ).start()
        return carry

    lax.fori_loop(1, nd, send_ids, 0)
    own_ids = pltpu.make_async_copy(table.at[me], ids.at[me], own_sem.at[0])
    own_ids.start()

    here = place_of(hd)

    def q_copies(peer, remote):
        nope_from = nope_out.at[:, pl.ds(pl.multiple_of(peer * heads, heads), heads), :]
        nope_to = nope_in.at[pl.ds(here, q_rows)]
        rope_to = rope_in.at[here // q_rows]
        if not remote:
            return [
                pltpu.make_async_copy(nope_from, nope_to, own_sem.at[1]),
                pltpu.make_async_copy(rope_out.at[peer], rope_to, own_sem.at[2]),
            ]
        return [
            pltpu.make_async_remote_copy(
                src_ref=nope_from, dst_ref=nope_to, send_sem=nope_send, recv_sem=nope_recv,
                device_id=(me, peer), device_id_type=MESH,
            ),
            pltpu.make_async_remote_copy(
                src_ref=rope_out.at[peer], dst_ref=rope_to, send_sem=rope_send, recv_sem=rope_recv,
                device_id=(me, peer), device_id_type=MESH,
            ),
        ]

    def send_q(step, carry):
        for copy in q_copies(lax.rem(hd + step, nh), True):
            copy.start()
        return carry

    lax.fori_loop(1, nh, send_q, 0)
    own_q = q_copies(hd, False)
    for copy in own_q:
        copy.start()

    loads[1].wait()
    own_ids.wait()
    wait_bytes(ids.at[pl.ds(0, nd - 1)], id_recv)
    expand = (iota((nd * part, nd), 0) // part == iota((nd * part, nd), 1)).astype(BF16)
    asked = jnp.dot(expand, ids[:, 0, :].astype(BF16), preferred_element_type=F32)
    offset = (lax.rem(iota((nd * part, 1), 0), part) + core * part).astype(F32)

    def row_copy(source, dest, send_sem, recv_sem, peer):
        return pltpu.make_async_remote_copy(
            src_ref=source.at[peer], dst_ref=dest.at[me], send_sem=send_sem, recv_sem=recv_sem,
            device_id=(peer, hd), device_id_type=MESH,
        )

    own_rows = []
    for slot, (source, dest, send_sem, recv_sem) in enumerate(
        [(out0, in0, send0, recv0), (out1, in1, send1, recv1)]
    ):
        wanted = asked[:, slot:slot + 1]
        target = jnp.where(wanted < 0.0, -1e6, wanted * pair) + offset
        picked = pick_rows(target, 0.0, rows_here[...].reshape(blocks * pair, width))
        source[...] = picked.astype(BF16).reshape(nd, part, width)

        def send_rows(step, carry, source=source, dest=dest, send_sem=send_sem, recv_sem=recv_sem):
            row_copy(source, dest, send_sem, recv_sem, lax.rem(me + step, nd)).start()
            return carry

        if slot == 0: lax.fori_loop(1, nd, send_rows, 0)
        own = pltpu.make_async_copy(source.at[me], dest.at[me], own_sem.at[3 + slot])
        own.start()
        own_rows.append(own)

    wait_bytes(in0.at[pl.ds(0, nd - 1)], send0)
    lax.fori_loop(1, nd, send_rows, 0)
    for copy in own_q:
        copy.wait()
    loads[2].wait()
    wait_bytes(nope_in.at[pl.ds(0, rows - q_rows)], nope_recv)
    wait_bytes(rope_in.at[pl.ds(0, nh - 1)], rope_recv)
    nope[...] = nope_in[...].reshape(rows * heads, nope_dim).astype(F32)
    rope[...] = rope_in[...].reshape(rows * half_heads, 2 * rope_dim).astype(F32)
    part_rows = pre // 2

    def put_query(h, columns, value):
        for side in range(2):
            at = pl.ds((side * heads + h) * part_rows, part_rows)
            query_p[at, columns] = value[side * part_rows:(side + 1) * part_rows]
        query_d[pl.ds(h * dec, dec), columns] = value[pre:]

    for h in range(heads):
        picked = nope[pl.ds(h, rows, stride=heads), :].astype(BF16)
        absorbed = jnp.dot(picked, key_up[h], preferred_element_type=F32).astype(BF16)
        put_query(h, slice(0, latent), absorbed)
    for h in range(half_heads):
        both = rope[pl.ds(h, rows, stride=half_heads), :].astype(BF16)
        put_query(h, slice(latent, width), both[:, :rope_dim])
        put_query(h + half_heads, slice(latent, width), both[:, rope_dim:])

    right, left = lax.rem(hd + 2, nh), lax.rem(hd - 2 + nh, nh)
    far = lax.rem(hd + nh // 2, nh)
    chunk_half = reqs * part // 4

    def share(keys, send_sem, recv_sem, index, side, peer, slot):
        span = keys.at[index, pl.ds(side * chunk_half, chunk_half)]
        return pltpu.make_async_remote_copy(
            src_ref=span, dst_ref=span, send_sem=send_sem.at[slot],
            recv_sem=recv_sem.at[index, side], device_id=(me, peer), device_id_type=MESH,
        )

    def share_own(*gang):
        for slot, (side, peer) in enumerate(
            [(0, right), (1, left), (1, right), (0, left), (0, sibling), (1, sibling)]
        ):
            share(*gang, hd, side, peer, slot).start()

    def landed(index, side, *gang):
        share(*gang, index, side, sibling, 0).wait_recv()

    def share_near(*gang):
        landed(left, 0, *gang)
        share(*gang, left, 0, right, 6).start()
        share(*gang, left, 0, sibling, 7).start()
        landed(right, 1, *gang)
        share(*gang, right, 1, left, 8).start()
        share(*gang, right, 1, sibling, 9).start()
        landed(left, 1, *gang)
        share(*gang, left, 1, sibling, 10).start()
        landed(right, 0, *gang)
        share(*gang, right, 0, sibling, 11).start()

    def share_far(*gang):
        for side in range(2):
            landed(far, side, *gang)
            share(*gang, far, side, sibling, 12 + side).start()

    def near_here(*gang):
        for step in (0, 2, nh - 2):
            for side in range(2):
                landed(lax.rem(sibling + step, nh), side, *gang)

    def far_here(*gang):
        for side in range(2):
            landed(lax.rem(sibling + nh // 2, nh), side, *gang)

    def share_sent(*gang):
        for slot in range(14):
            share(*gang, hd, 0, sibling, slot).wait_send()

    gang_a = (keys_a, a_send, a_recv)
    gang_b = (keys_b, b_send, b_recv)

    def give(device):
        source = values_out.at[pl.ds(pl.multiple_of(place_of(jnp.int32(device)), 4), q_rows)]
        dest = out_ref.at[:, pl.ds(pl.multiple_of(hd * heads, heads), heads), :]

        @pl.when(hd != device)
        def _():
            pltpu.make_async_remote_copy(
                src_ref=source, dst_ref=dest, send_sem=out_send, recv_sem=out_recv,
                device_id=(me, device), device_id_type=MESH,
            ).start()

        @pl.when(hd == device)
        def _():
            pltpu.make_async_copy(source, dest, own_sem.at[5]).start()

    def put_values(first, count, mixed, base):
        for h in range(heads):
            values[pl.ds(first * heads + h, count, stride=heads), :] = jnp.dot(
                mixed[pl.ds(base + h * count, count), :], value_up[h], preferred_element_type=F32
            )
        done = values[pl.ds(first * heads, count * heads), :].astype(BF16)
        values_out[pl.ds(first, count)] = done.reshape(count, heads, done.shape[1])

    own_rows[0].wait()
    wait_bytes(in0.at[pl.ds(0, nd - 1)], recv0)
    first_rows = in0[...].reshape(nd * part, width)
    keys_a[hd] = pick_rows(spread_rows(early, part), 0.0, first_rows).astype(BF16)
    share_own(*gang_a)

    loads[3].wait()
    loads[4].wait()
    eye = iota((dec, dec), 0) == iota((dec, dec), 1)
    start = jnp.sum(jnp.where(eye, start_ref[...].astype(F32), 0.0), axis=1, keepdims=True)
    length = jnp.sum(jnp.where(eye, length_ref[...].astype(F32), 0.0), axis=1, keepdims=True)
    place = iota((dec, pool), 1).astype(F32) - start
    seen[...] = jnp.where((place >= 0.0) & (place < length), 0.0, HIDDEN)
    step_blocks = blocks // 4
    step_keys = step_blocks * block_rows
    size_d = heads * dec

    def decode_block(index, carry):
        at = pl.ds(pl.multiple_of(index * size_d, size_d), size_d)
        query = query_d[at, :]
        local = latents[rows - pre:, :]
        own = lax.rem(iota((size_d, pre), 0), dec) + (pre - dec)
        kept = [jnp.where(iota((size_d, pre), 1) == own, scores(query, local), HIDDEN)]
        held = [local]
        for j in range(4):
            keys = cache[j * step_blocks:(j + 1) * step_blocks].reshape(step_keys, width)
            one = scores(query, keys).reshape(size_d // dec, dec, step_keys)
            one = one + seen[:, j * step_keys:(j + 1) * step_keys][None]
            kept.append(one.reshape(size_d, step_keys))
            held.append(keys)
        top = functools.reduce(jnp.maximum, [jnp.max(x, axis=1, keepdims=True) for x in kept]) * exponent
        weight, mixed = 0.0, 0.0
        for x, keys in zip(kept, held):
            raised = jnp.exp2(x * exponent - top)
            weight += jnp.sum(raised, axis=1, keepdims=True)
            mixed += jnp.dot(raised.astype(BF16), keys[:, :latent], preferred_element_type=F32)
        mixed_d[at, :] = (mixed / weight).astype(BF16)
        return carry

    decode_block(0, 0)
    loads[5].wait()
    put_values(pre, dec, mixed_d, 0)
    give(nh - 1)

    share_near(*gang_a)

    own_rows[1].wait()
    wait_bytes(in1.at[pl.ds(0, nd - 1)], recv1)
    target = spread_rows(late, part)
    keys_b[hd] = (
        pick_rows(target, 0.0, in0[...].reshape(nd * part, width))
        + pick_rows(target, float(nd * part), in1[...].reshape(nd * part, width))
    ).astype(BF16)
    share_own(*gang_b)

    share_far(*gang_a)
    near_here(*gang_a)
    far_here(*gang_a)

    size = heads * part_rows // 2

    pieces = 2
    piece = nh // pieces

    def soften(kept, held, top):
        weight, mixed = 0.0, 0.0
        for x, keys in zip(kept, held):
            raised = jnp.exp2(x * exponent - top)
            weight += jnp.sum(raised, axis=1, keepdims=True)
            mixed += jnp.dot(raised.astype(BF16), keys[:, :latent], preferred_element_type=F32)
        return weight, mixed

    def highest(kept):
        return functools.reduce(jnp.maximum, [jnp.max(x, axis=1, keepdims=True) for x in kept]) * exponent

    def early_block(index, carry):
        at = pl.ds(pl.multiple_of(index * size, size), size)
        query = query_p[at, :]
        side = pl.ds(pl.multiple_of(index // 2 * part_rows, part_rows), part_rows)
        held = [keys_a[j * piece:(j + 1) * piece].reshape(-1, width) for j in range(pieces)]
        kept = [scores(query, keys) for keys in held]
        held.append(latents[:pre, :])
        own = scores(query, held[-1]).reshape(size // part_rows, part_rows, pre) + causal[side, :][None]
        kept.append(own.reshape(size, pre))
        top = highest(kept)
        weight, mixed = soften(kept, held, top)
        acc[at, :] = mixed
        peak[at, :] = jnp.broadcast_to(top, (size, 128))
        total[at, :] = jnp.broadcast_to(weight, (size, 128))
        return carry

    def late_block(index, carry):
        at = pl.ds(pl.multiple_of(index * size, size), size)
        query = query_p[at, :]
        held = [keys_b[j * piece:(j + 1) * piece].reshape(-1, width) for j in range(pieces)]
        kept = [scores(query, keys) for keys in held]
        old = peak[at, :][:, 0:1]
        top = jnp.maximum(old, highest(kept))
        fix = jnp.exp2(old - top)
        weight, mixed = soften(kept, held, top)
        weight += total[at, :][:, 0:1] * fix
        mixed_p[at, :] = ((acc[at, :] * fix + mixed) / weight).astype(BF16)
        return carry

    lax.fori_loop(0, 2, early_block, 0, unroll=True)
    share_near(*gang_b)
    lax.fori_loop(2, 4, early_block, 0, unroll=True)
    share_far(*gang_b)
    near_here(*gang_b)
    far_here(*gang_b)
    lax.fori_loop(0, 2, late_block, 0, unroll=True)
    put_values(0, part_rows, mixed_p, 0)
    for device in range(0, 2 * front, 2):
        give(device)
    lax.fori_loop(2, 4, late_block, 0, unroll=True)
    put_values(part_rows, part_rows, mixed_p, heads * part_rows)
    for device in [*range(1, 2 * front, 2), *range(2 * front, nh - 1)]:
        give(device)

    share_sent(*gang_a)
    share_sent(*gang_b)
    wait_bytes(nope_in.at[pl.ds(0, rows - q_rows)], nope_send)
    wait_bytes(rope_in.at[pl.ds(0, nh - 1)], rope_send)
    wait_bytes(in1.at[pl.ds(0, nd - 1)], send1)
    wait_bytes(table.at[pl.ds(0, nd - 1)], id_send)
    wait_bytes(values_out.at[pl.ds(0, q_rows)], own_sem.at[5])
    wait_bytes(values_out.at[pl.ds(0, rows - q_rows)], out_send)
    wait_bytes(values_out.at[pl.ds(0, rows - q_rows)], out_recv)


def body(
    queries, latents, cache_pool, key_up, value_up, prefix_rank, prefix_block, decode_start, decode_length
):
    nd, nh = lax.axis_size("dp"), lax.axis_size("head")
    q_rows, all_heads, q_width = queries.shape
    heads, nope_dim, latent = key_up.shape
    rows = q_rows * nh
    blocks, block_rows, width = cache_pool.shape
    part = block_rows // nh
    pair = CAP * part
    reqs = prefix_block.shape[0]
    dec = decode_start.shape[0]
    pre = rows - dec
    v_dim = value_up.shape[2]
    anywhere = pl.BlockSpec(memory_space=pl.ANY)
    vmem = pl.BlockSpec(memory_space=pltpu.VMEM)
    dma = pltpu.SemaphoreType.DMA
    half_keys = (nh, reqs // 2 * part, width)
    half_heads = heads // 2
    buffers = [
        ((q_rows, q_width, all_heads), BF16),
        (latents.shape, BF16),
        (cache_pool.shape, BF16),
        (key_up.shape, BF16),
        (value_up.shape, BF16),
        ((blocks, pair, width), BF16),
        ((nd, 1, 128), F32),
        ((nd, 1, 128), F32),
        ((q_rows, all_heads, nope_dim), BF16),
        ((nh, q_rows * half_heads, 2 * (q_width - nope_dim)), BF16),
        ((rows, heads, nope_dim), BF16),
        ((nh, q_rows * half_heads, 2 * (q_width - nope_dim)), BF16),
        ((rows * heads, nope_dim), F32),
        ((rows * half_heads, 2 * (q_width - nope_dim)), F32),
        ((nd, part, width), BF16),
        ((nd, part, width), BF16),
        ((nd, part, width), BF16),
        ((nd, part, width), BF16),
        (half_keys, BF16),
        (half_keys, BF16),
        ((pre * heads, width), BF16),
        ((dec * heads, width), BF16),
        ((pre * heads, latent), BF16),
        ((dec * heads, latent), BF16),
        ((rows * heads, v_dim), F32),
        ((rows, heads, v_dim), BF16),
        ((dec, blocks * block_rows), F32),
        ((pre * heads, latent), F32),
        ((pre * heads, 128), F32),
        ((pre * heads, 128), F32),
        ((pre, pre), F32),
    ]
    return pl.pallas_call(
        kernel,
        out_shape=jax.ShapeDtypeStruct((q_rows, all_heads, v_dim), BF16),
        in_specs=[anywhere] * 5 + [vmem] * 4,
        out_specs=anywhere,
        scratch_shapes=[pltpu.VMEM(shape, dtype) for shape, dtype in buffers]
        + [dma((6,))] + [dma] * 10 + [dma((14,)), dma((nh, 2))] * 2 + [dma, dma, dma((6,))],
        compiler_params=pltpu.CompilerParams(
            collective_id=0, has_side_effects=True, vmem_limit_bytes=60 * 2**20
        ),
        name="serve",
    )(
        jnp.swapaxes(queries, 1, 2), latents, cache_pool, key_up, value_up,
        prefix_rank.reshape(1, reqs), prefix_block.reshape(1, reqs),
        decode_start.reshape(1, dec), decode_length.reshape(1, dec),
    )


def solution(mesh):
    return jax.shard_map(
        body,
        mesh=mesh,
        in_specs=(
            P(("dp", "head"), None, None),
            P("dp", None),
            P("dp", None, None),
            P("head", None, None),
            P("head", None, None),
            P("dp", None),
            P("dp"),
            P("dp"),
            P("dp"),
        ),
        out_specs=P(("dp", "head"), None, None),
        check_vma=False,
    )
```
